256 devices in a mesh: pts: 64 (over z, x_hi, y), dim: 4 (over x_lo, core).
Axes of the slice: x: 4 (x_hi: 2, x_lo: 2; x = x_hi * 2 + x_lo), y: 4, z: 8, core: 2. Of those that a mesh axis runs over, the one named last changes fastest.
Arguments:
- points: bfloat16 [40960, 1024], P('pts', 'dim'), may hold values from -0.46875 to 0.46875
- grad_weights: bfloat16 [40960, 1024], P('pts', 'dim'), may hold values from -6 to 6
- value_weights: bfloat16 [40960], P('pts'), may hold values from -12 to 12
Outputs:
- value_product: float32 [40960], P('pts')
- grad_product: float32 [40960, 1024], P('pts', 'dim')
The draws below stay inside these ranges and needn't reach their ends.
All inputs are finite; a program needn't handle non-finite values.
Results may differ from the reference program's by a relative error of at most 0.0027.
Values may be sent and summed in bfloat16 or wider, within the bound.
No kernel may reach another device: no remote copies, remote signals or barrier semaphores. Data moves between devices by JAX's collectives and lax.ppermute only.
A program may use at most 64 MiB of HBM per device.

```python
import jax
import jax.numpy as jnp
from jax import lax

D = 1024
PTS_DEV = 640
ROUNDS = 3
POINTS = 40960
N_PTS = 64


def draw_points(key, part):
    key = jax.random.fold_in(key, 17)
    key_latent, key_gain, key_jitter = jax.random.split(key, 3)
    column_gain = jax.random.uniform(key_gain, (D,), jnp.float32, 0.5, 1.5)
    latent = jax.random.truncated_normal(key_latent, -4.0, 4.0, (POINTS, 8), jnp.float32)
    jitter = jax.random.truncated_normal(key_jitter, -4.0, 4.0, (POINTS, D), jnp.float32)
    spread = jnp.tile(latent, (1, D // 8))
    values = (3.0 / D) ** 0.5 * column_gain[None, :] * spread + (1.0 / D) ** 0.5 * jitter
    return values.astype(jnp.bfloat16)


def levels(stream_key, dims, cuts, low, high):
    factor_of = 1.0
    for dim, blocks in cuts:
        steps = jax.random.uniform(jax.random.fold_in(jax.random.fold_in(stream_key, 6), dim), (blocks,), jnp.float32, low / len(cuts), high / len(cuts))
        factor_of = factor_of * jnp.repeat(jnp.exp(steps), dims[dim] // blocks).reshape((-1,) + (1,) * (len(dims) - 1 - dim))
    return factor_of


def centred(stream_key, shape, scale, most, cuts=(), kind=jnp.bfloat16):
    values = scale * jax.random.normal(stream_key, shape, jnp.float32)
    if cuts:
        values = values * levels(stream_key, shape, cuts, -0.22, 0.18)
    return jnp.clip(values, -most, most).astype(kind)


def setup_inputs(seed: int = 0) -> dict:
    key_of = jax.random.split(jax.random.key(seed), 4)
    return {
        "points": draw_points(jax.random.fold_in(key_of[3], 71), 0),
        "grad_weights": centred(key_of[1], (POINTS, D), 1.0, 6.0, ((0, 64), (1, 4))),
        "value_weights": centred(key_of[2], (POINTS,), 2.0, 12.0, ((0, 64),)),
    }


def pair_terms(own_u, own_b, far_u, far_b, far_a):
    own32 = own_u.astype(jnp.float32)
    far32 = far_u.astype(jnp.float32)
    own_norm = jnp.sum(own32 * own32, 1)
    far_norm = jnp.sum(far32 * far32, 1)
    far_inner = jnp.sum(far32 * far_b.astype(jnp.float32), 1)
    gram = jnp.dot(own_u, far_u.T, preferred_element_type=jnp.float32)
    cross = jnp.dot(own_u, far_b.T, preferred_element_type=jnp.float32)
    kern = jnp.exp(-0.5 * (own_norm[:, None] + far_norm[None, :] - 2.0 * gram))
    weight = -kern * (far_a.astype(jnp.float32)[None, :] + cross - far_inner[None, :])
    rowsum = jnp.sum(weight, 1)
    grad = own32 * rowsum[:, None] - jnp.dot(weight.astype(jnp.bfloat16), far_u, preferred_element_type=jnp.float32) + jnp.dot(kern.astype(jnp.bfloat16), far_b, preferred_element_type=jnp.float32)
    return -rowsum, grad


def reference(points, grad_weights, value_weights):
    blocks_u = points.reshape(N_PTS, PTS_DEV, D)
    blocks_b = grad_weights.reshape(N_PTS, PTS_DEV, D)
    blocks_a = value_weights.reshape(N_PTS, PTS_DEV)

    def one_block(index):
        own_u = blocks_u[index]
        own_b = blocks_b[index]
        value, grad = pair_terms(own_u, own_b, own_u, own_b, blocks_a[index])
        for bit in range(ROUNDS):
            other = jnp.bitwise_xor(index, jnp.int32(1 << bit))
            more_value, more_grad = pair_terms(own_u, own_b, blocks_u[other], blocks_b[other], blocks_a[other])
            value = value + more_value
            grad = grad + more_grad
        return value, grad

    values, grads = lax.map(one_block, jnp.arange(N_PTS, dtype=jnp.int32))
    return values.reshape(POINTS), grads.reshape(POINTS, D)
```

```python
import functools

import jax
import jax.numpy as jnp
from jax import lax
from jax.experimental import pallas as pl
from jax.experimental.pallas import tpu as pltpu
from jax.sharding import PartitionSpec as P

F32, BF16 = jnp.float32, jnp.bfloat16
VMEM = pl.BlockSpec(memory_space=pltpu.VMEM)
NT = (((1,), (1,)), ((), ()))


def permute(array, pts, dim):
    devices_p, devices_d = lax.axis_size("pts"), lax.axis_size("dim")
    pairs = [
        (p * devices_d + d, (p ^ pts) * devices_d + (d ^ dim))
        for p in range(devices_p)
        for d in range(devices_d)
    ]
    return lax.ppermute(array, ("pts", "dim"), pairs)


def call(kernel, outs, *args, flops=0, moved=0):
    return pl.pallas_call(
        kernel,
        out_shape=outs,
        in_specs=[VMEM] * len(args),
        out_specs=[VMEM] * len(outs),
        compiler_params=pltpu.CompilerParams(vmem_limit_bytes=16 << 20),
        cost_estimate=pl.CostEstimate(flops=flops, bytes_accessed=moved, transcendentals=0),
    )(*args)


def shape(rows, cols, dtype=BF16):
    return jax.ShapeDtypeStruct((rows, cols), dtype)


def quarter(ref, which, size):
    return ref[pl.ds(pl.multiple_of(which * size, 16), size), :]


def pack(share, u, b, core, chip, cross):
    rows, me = u.shape[0], lax.axis_index("dim")
    core[:rows] = u[...]
    core[rows:] = quarter(b, me ^ 1, share)
    chip[:share] = quarter(u, me ^ 2, share)
    chip[share:] = quarter(b, me ^ 2, share)
    cross[:share] = quarter(u, me ^ 3, share)
    cross[share:] = quarter(b, me ^ 3, share)


def lay_near(share, u, b, core, coef, near):
    rows, me = u.shape[0], lax.axis_index("dim")
    near[:share] = quarter(u, me, share)
    near[share : 2 * share] = quarter(b, me, share)
    near[2 * share : 3 * share] = quarter(core, me, share)
    near[3 * share : 4 * share] = core[rows:]
    row = lax.broadcasted_iota(jnp.int32, coef.shape, 0)
    mine = jnp.sum(jnp.where(row == me, coef[...], 0.0), 0, keepdims=True)
    near[4 * share :] = jnp.broadcast_to(mine, (16, mine.shape[1])).astype(BF16)


def lay_far(chip, cross, far):
    half = chip.shape[0]
    far[:half] = chip[...]
    far[half:] = cross[...]


def as_row(column):
    size = column.shape[0]
    diagonal = lax.broadcasted_iota(jnp.int32, (size, size), 0) == lax.broadcasted_iota(
        jnp.int32, (size, size), 1
    )
    return jnp.sum(jnp.where(diagonal, column, 0.0), 0, keepdims=True)


def norms_of(slices):
    total = 0.0
    for part in slices:
        wide = part.astype(F32)
        total = total + wide * wide
    return jnp.sum(total, 1, keepdims=True)


def meet(share, own, own_norm, near, far):
    far_u = [near[:share], near[2 * share : 3 * share], far[:share], far[2 * share : 3 * share]]
    far_b = [near[share : 2 * share], near[3 * share : 4 * share], far[share : 2 * share], far[3 * share :]]
    inner = 0.0
    for part_u, part_b in zip(far_u, far_b):
        inner = inner + part_u.astype(F32) * part_b.astype(F32)
    inner = as_row(jnp.sum(inner, 1, keepdims=True))
    norm = as_row(norms_of(far_u))
    coef = near[4 * share :].astype(F32)[:1, :share]
    gram = cross = 0.0
    for mine, part_u, part_b in zip(own, far_u, far_b):
        gram = gram + lax.dot_general(mine, part_u, NT, preferred_element_type=F32)
        cross = cross + lax.dot_general(mine, part_b, NT, preferred_element_type=F32)
    kern = jnp.exp(gram - 0.5 * (own_norm + norm))
    minus = kern * (coef + cross - inner)
    return kern.astype(BF16), minus, far_u, far_b


def contribution(k, own, kern_b, minus_b, value, far_u, far_b):
    return (
        jnp.dot(minus_b, far_u[k], preferred_element_type=F32)
        + jnp.dot(kern_b, far_b[k], preferred_element_type=F32)
        - own[k].astype(F32) * value
    )


def first_meet(share, u, core, chip_u, cross_u, near, far, near_y, far_y, near_x, far_x, grad, value):
    rows = u.shape[0]
    own = [u[...], core[:rows], chip_u[...], cross_u[...]]
    own_norm = norms_of(own)
    total = 0.0
    for turn, (block_near, block_far) in enumerate(((near, far), (near_y, far_y), (near_x, far_x))):
        flip = 2 if turn == 2 else 0
        turned = [own[k ^ flip] for k in range(4)]
        kern_b, minus, far_u, far_b = meet(share, turned, own_norm, block_near, block_far)
        part = jnp.sum(minus, 1, keepdims=True)
        total = total + part
        minus_b = minus.astype(BF16)
        for k in range(4):
            term = contribution(k, turned, kern_b, minus_b, part, far_u, far_b)
            at = pl.ds((k ^ flip) * rows, rows)
            grad[at, :] = term if turn == 0 else grad[at, :] + term
    value[...] = jnp.broadcast_to(total, value.shape)


def put_values(out, start, rows_of):
    high = rows_of.astype(BF16)
    low = (rows_of - high.astype(F32)).astype(BF16)
    out[start:] = jnp.concatenate([high, low], 1)


def take_values(ref, start):
    both = ref[start:].astype(F32)
    half = both.shape[1] // 2
    return both[:, :half] + both[:, half:]


def last_meet(share, u, core, chip_u, cross_u, near, far, grad, value, send, keep):
    rows = u.shape[0]
    own = [u[...], core[:rows], chip_u[...], cross_u[...]]
    own_norm = norms_of(own)
    kern_b, minus, far_u, far_b = meet(share, own, own_norm, near, far)
    part = jnp.sum(minus, 1, keepdims=True)
    minus_b = minus.astype(BF16)
    for k in (1, 3, 0, 2):
        term = grad[k * rows : (k + 1) * rows] + contribution(
            k, own, kern_b, minus_b, part, far_u, far_b
        )
        at = pl.ds((k // 2) * rows, rows)
        if k % 2:
            send[at, :] = term.astype(BF16)
        else:
            keep[at, :] = term
    total = value[:, :1] + part
    lines = [as_row(total[at : at + 128]) for at in range(0, rows, 128)]
    lines += [jnp.zeros_like(lines[0])] * (16 - len(lines))
    lines = jnp.concatenate(lines, 0)
    put_values(send, 2 * rows, lines)
    keep[2 * rows :, :] = jnp.concatenate([lines, jnp.zeros_like(lines)], 1)


def sum_cores(rows, keep, back, send):
    send[:rows] = (keep[rows : 2 * rows] + back[rows : 2 * rows].astype(F32)).astype(BF16)
    put_values(send, rows, keep[2 * rows :, :128] + take_values(back, 2 * rows))


def sum_chips(rows, keep, back, far, grad, value):
    grad[...] = keep[:rows] + back[:rows].astype(F32) + far[:rows].astype(F32)
    total = keep[2 * rows :, :128] + take_values(back, 2 * rows) + take_values(far, rows)
    value[...] = total[: value.shape[0]]


def body(points, grad_weights, value_weights):
    rows, cols = points.shape
    share = rows // lax.axis_size("dim")
    coef = value_weights.astype(F32).reshape(rows // share, share)
    coef = jnp.pad(coef, ((0, 0), (0, cols - share)))

    core, chip, cross = call(
        functools.partial(pack, share),
        [shape(rows + share, cols), shape(2 * share, cols), shape(2 * share, cols)],
        points,
        grad_weights,
    )
    core = permute(core, 0, 1)
    chip = permute(chip, 0, 2)
    cross = permute(cross, 0, 3)
    near = call(
        functools.partial(lay_near, share),
        [shape(4 * share + 16, cols)],
        points,
        grad_weights,
        core,
        coef,
    )[0]
    near_y = permute(near, 1, 0)
    near_x = permute(near, 4, 2)
    chip_u = permute(points, 0, 2)
    far = call(lay_far, [shape(4 * share, cols)], chip, cross)[0]
    near_yy = permute(near_y, 3, 0)
    far_y = permute(far, 1, 0)
    far_x = permute(far, 4, 2)
    cross_u = permute(chip_u, 0, 1)
    far_yy = permute(far_y, 3, 0)

    dots = 4 * 2 * rows * share * 4 * cols
    grad, value = call(
        functools.partial(first_meet, share),
        [shape(4 * rows, cols, F32), shape(rows, 128, F32)],
        points,
        core,
        chip_u,
        cross_u,
        near,
        far,
        near_y,
        far_y,
        near_x,
        far_x,
        flops=3 * dots,
    )
    send, keep = call(
        functools.partial(last_meet, share),
        [shape(2 * rows + 16, cols), shape(2 * rows + 16, cols, F32)],
        points,
        core,
        chip_u,
        cross_u,
        near_yy,
        far_yy,
        grad,
        value,
        flops=dots,
    )
    back = permute(send, 0, 1)
    send = call(functools.partial(sum_cores, rows), [shape(rows + 16, cols)], keep, back)[0]
    far_sum = permute(send, 0, 2)
    grad, value = call(
        functools.partial(sum_chips, rows),
        [shape(rows, cols, F32), shape(rows // 128, 128, F32)],
        keep,
        back,
        far_sum,
    )
    return value.reshape(rows), grad


def solution(mesh):
    return jax.shard_map(
        body,
        mesh=mesh,
        in_specs=(P("pts", "dim"), P("pts", "dim"), P("pts")),
        out_specs=(P("pts"), P("pts", "dim")),
        check_vma=False,
    )
```

```python
import functools

import jax
import jax.numpy as jnp
from jax import lax
from jax.experimental import pallas as pl
from jax.experimental.pallas import tpu as pltpu
from jax.sharding import PartitionSpec as P

F32, BF16 = jnp.float32, jnp.bfloat16
VMEM = pl.BlockSpec(memory_space=pltpu.VMEM)
ANY = pl.BlockSpec(memory_space=pltpu.HBM)
NT = (((1,), (1,)), ((), ()))


def permute(array, pts, dim):
    devices_p, devices_d = lax.axis_size("pts"), lax.axis_size("dim")
    pairs = [
        (p * devices_d + d, (p ^ pts) * devices_d + (d ^ dim))
        for p in range(devices_p)
        for d in range(devices_d)
    ]
    return lax.ppermute(array, ("pts", "dim"), pairs)


def call(kernel, outs, *args, flops=0, scratch=(), spec=VMEM):
    return pl.pallas_call(
        kernel,
        out_shape=outs,
        in_specs=[spec] * len(args),
        out_specs=[VMEM] * len(outs),
        scratch_shapes=scratch,
        compiler_params=pltpu.CompilerParams(vmem_limit_bytes=16 << 20),
        cost_estimate=pl.CostEstimate(flops=flops, bytes_accessed=0, transcendentals=0),
    )(*args)


def shape(rows, cols, dtype=BF16):
    return jax.ShapeDtypeStruct((rows, cols), dtype)


def quarter(which, size):
    return pl.ds(pl.multiple_of(which * size, 16), size)


def pack(share, u, b, whole, chip, cross, own, sems):
    rows, me = u.shape[0], lax.axis_index("dim")
    upper = pl.ds(0, share)
    lower = pl.ds(share, share)
    moves = [(u, whole.at[pl.ds(0, rows)]), (b.at[quarter(me ^ 1, share)], whole.at[pl.ds(rows, share)])]
    for which, out in ((2, chip), (3, cross), (0, own)):
        moves.append((u.at[quarter(me ^ which, share)], out.at[upper]))
        moves.append((b.at[quarter(me ^ which, share)], out.at[lower]))
    copies = [pltpu.make_async_copy(*move, sems.at[n]) for n, move in enumerate(moves)]
    for copy in copies:
        copy.start()
    for copy in copies:
        copy.wait()


def lay_near(share, own, core, coef, near):
    rows, me = core.shape[0] - share, lax.axis_index("dim")
    near[: 2 * share] = own[...]
    near[2 * share : 3 * share] = core[quarter(me, share), :]
    near[3 * share : 4 * share] = core[rows:]
    lanes = coef.shape[1]
    row = lax.broadcasted_iota(jnp.int32, coef.shape, 0)
    first, skip = me * share // lanes, me * share % lanes
    parts = [
        jnp.sum(jnp.where(row == first + n, coef[...], 0.0), 0, keepdims=True) for n in range(2)
    ]
    mine = jnp.broadcast_to(jnp.concatenate(parts, 1), (16, 2 * lanes))
    near[4 * share :] = pltpu.roll(mine, lax.rem(2 * lanes - skip, 2 * lanes), 1).astype(BF16)


def lay_far(share, chip, cross, near, far, both):
    far[: 2 * share] = chip[...]
    far[2 * share :] = cross[...]
    both[: 4 * share] = far[...]
    both[4 * share :] = near[...]


def lay_half(share, whole, *refs):
    half = refs[-1]
    half[...] = whole[quarter(lax.axis_index("dim") // 2, 2 * share), :]


def lay_rest(share, far, half, rest):
    rest[:share] = far[:share]
    rest[share : 2 * share] = far[2 * share : 3 * share]
    rest[2 * share :] = half[...]


def as_row(column):
    size = column.shape[0]
    diagonal = lax.broadcasted_iota(jnp.int32, (size, size), 0) == lax.broadcasted_iota(
        jnp.int32, (size, size), 1
    )
    return jnp.sum(jnp.where(diagonal, column, 0.0), 0, keepdims=True)


def norms_of(slices):
    total = 0.0
    for part in slices:
        wide = part.astype(F32)
        total = total + wide * wide
    return jnp.sum(total, 1, keepdims=True)


def halves(share, ref):
    return ref.at[: 2 * share], ref.at[2 * share : 4 * share]


def meet(share, own, own_norm, pieces, coef):
    far_u = [piece[:share] for piece in pieces]
    far_b = [piece[share : 2 * share] for piece in pieces]
    inner = 0.0
    for part_u, part_b in zip(far_u, far_b):
        inner = inner + part_u.astype(F32) * part_b.astype(F32)
    inner = as_row(jnp.sum(inner, 1, keepdims=True))
    norm = as_row(norms_of(far_u))
    coef = coef[4 * share :].astype(F32)[:1, :share]
    gram = cross = 0.0
    for mine, part_u, part_b in zip(own, far_u, far_b):
        gram = gram + lax.dot_general(mine[...], part_u, NT, preferred_element_type=F32)
        cross = cross + lax.dot_general(mine[...], part_b, NT, preferred_element_type=F32)
    kern = jnp.exp(gram - 0.5 * (own_norm + norm))
    minus = kern * (coef + cross - inner)
    return kern, minus


def contribution(share, own, kern_b, minus_b, value, piece):
    return (
        jnp.dot(minus_b, piece[:share], preferred_element_type=F32)
        + jnp.dot(kern_b, piece[share : 2 * share], preferred_element_type=F32)
        - own[...].astype(F32) * value
    )


def meet_own(share, *refs):
    whole, core, near, far, half, rest, chip_u, cross_u, norm, grad, value = refs
    rows, me = whole.shape[0] - share, lax.axis_index("dim")
    other = quarter(1 - me // 2, 2 * share)
    chip, cross = halves(share, far)
    chip_u[quarter(me, share), :] = chip[:share]
    chip_u[quarter(me ^ 1, share), :] = rest[share : 2 * share]
    chip_u[other, :] = half[...]
    cross_u[quarter(me, share), :] = cross[:share]
    cross_u[quarter(me ^ 1, share), :] = rest[:share]
    cross_u[other, :] = rest[2 * share :]
    own = [whole[:rows], core[:rows], chip_u[...], cross_u[...]]
    own_norm = norms_of(own)
    norm[...] = jnp.broadcast_to(own_norm, norm.shape)
    pieces = [*halves(share, near), *halves(share, far)]
    kern, minus = meet(share, own, own_norm, pieces, near)
    total = jnp.sum(minus, 1, keepdims=True)
    value[...] = jnp.broadcast_to(total, value.shape)
    kern_b, minus_b = kern.astype(BF16), minus.astype(BF16)
    for k in range(4):
        grad[k * rows : (k + 1) * rows] = contribution(share, own[k], kern_b, minus_b, total, pieces[k])


def add_block(share, own, norm, pieces, coef, grad_in, value_in, grad, value):
    rows = norm.shape[0]
    kern, minus = meet(share, own, norm[:, :1], pieces, coef)
    total = jnp.sum(minus, 1, keepdims=True)
    value[...] = value_in[...] + total
    kern_b, minus_b = kern.astype(BF16), minus.astype(BF16)
    for k in range(4):
        at = slice(k * rows, (k + 1) * rows)
        grad[at] = grad_in[at] + contribution(share, own[k], kern_b, minus_b, total, pieces[k])


def meet_next(share, whole, core, chip_u, cross_u, norm, p01, p23, grad_in, value_in, grad, value):
    rows = norm.shape[0]
    own = [whole[:rows], core[:rows], chip_u[...], cross_u[...]]
    add_block(share, own, norm, [*halves(share, p01), *halves(share, p23)], p01, grad_in, value_in, grad, value)


def meet_across(share, *refs):
    whole, core, chip_u, cross_u, norm, both, grad_in, value_in, grad, value = refs
    rows = norm.shape[0]
    own = [whole[:rows], core[:rows], chip_u[...], cross_u[...]]
    p01 = both.at[4 * share :]
    add_block(share, own, norm, [*halves(share, both), *halves(share, p01)], p01, grad_in, value_in, grad, value)


def put_values(out, start, rows_of):
    high = rows_of.astype(BF16)
    low = (rows_of - high.astype(F32)).astype(BF16)
    out[start:] = jnp.concatenate([high, low], 1)


def take_values(ref, start):
    both = ref[start:].astype(F32)
    half = both.shape[1] // 2
    return both[:, :half] + both[:, half:]


def meet_last(share, *refs):
    whole, core, chip_u, cross_u, norm, p01, p23, grad, value_in, send, kern_b, minus_b, total, lines = refs
    rows = whole.shape[0] - share
    own = [whole[:rows], core[:rows], chip_u[...], cross_u[...]]
    kern, minus = meet(share, own, norm[:, :1], [*halves(share, p01), *halves(share, p23)], p01)
    part = jnp.sum(minus, 1, keepdims=True)
    kern_b[...] = kern.astype(BF16)
    minus_b[...] = minus.astype(BF16)
    total[...] = jnp.broadcast_to(part, total.shape)
    term = contribution(share, cross_u, kern_b[...], minus_b[...], part, halves(share, p23)[1])
    send[:rows] = (grad[3 * rows :] + term).astype(BF16)
    value = value_in[:, :1] + part
    rows_of = [as_row(value[at : at + 128]) for at in range(0, rows, 128)]
    rows_of += [jnp.zeros_like(rows_of[0])] * (16 - len(rows_of))
    lines[...] = jnp.concatenate(rows_of, 0)
    put_values(send, rows, lines[...])


def finish_chip(share, chip_u, kern_b, minus_b, total, p23, grad, out):
    rows = chip_u.shape[0]
    term = contribution(share, chip_u, kern_b[...], minus_b[...], total[:, :1], halves(share, p23)[0])
    out[...] = grad[2 * rows : 3 * rows] + term


def finish_core(share, core, kern_b, minus_b, total, p01, grad, send):
    rows = core.shape[0] - share
    term = contribution(share, core.at[:rows], kern_b[...], minus_b[...], total[:, :1], halves(share, p01)[1])
    send[...] = (grad[rows : 2 * rows] + term).astype(BF16)


def finish_own(share, whole, kern_b, minus_b, total, p01, grad, out):
    rows = whole.shape[0] - share
    term = contribution(share, whole.at[:rows], kern_b[...], minus_b[...], total[:, :1], halves(share, p01)[0])
    out[...] = grad[:rows] + term


def sum_cores(rows, keep, lines, back, send, both):
    send[:rows] = (keep[...] + back[:rows].astype(F32)).astype(BF16)
    both[...] = lines[...] + take_values(back, rows)
    put_values(send, rows, both[...])


def sum_chips(rows, keep, back, far, both, grad, value):
    grad[...] = keep[...] + back[...].astype(F32) + far[:rows].astype(F32)
    total = both[...] + take_values(far, rows)
    value[...] = total[: value.shape[0]]


def body(points, grad_weights, value_weights):
    rows, cols = points.shape
    share = rows // lax.axis_size("dim")
    piece = shape(2 * share, cols)
    part = functools.partial
    coef = value_weights.astype(F32).reshape(rows // 128, 128)

    whole, chip, cross, p0 = call(
        part(pack, share),
        [shape(rows + share, cols), piece, piece, piece],
        pltpu.with_memory_space_constraint(points, pltpu.HBM),
        pltpu.with_memory_space_constraint(grad_weights, pltpu.HBM),
        scratch=[pltpu.SemaphoreType.DMA((8,))],
        spec=ANY,
    )
    core = permute(whole, 0, 1)
    p2 = permute(chip, 0, 2)
    p3 = permute(cross, 0, 3)
    near01 = call(part(lay_near, share), [shape(4 * share + 16, cols)], p0, core, coef)[0]
    next01 = permute(near01, 1, 0)
    far, both = call(
        part(lay_far, share), [shape(4 * share, cols), shape(8 * share + 16, cols)], p2, p3, near01
    )
    next23 = permute(far, 1, 0)
    half = permute(call(part(lay_half, share), [piece], whole, far)[0], 0, 2)
    last01 = permute(next01, 3, 0)
    across = permute(both, 4, 2)
    rest = call(part(lay_rest, share), [shape(4 * share, cols)], far, half)[0]
    rest = permute(rest, 0, 1)
    last23 = permute(next23, 3, 0)

    sums = [shape(4 * rows, cols, F32), shape(rows, 128, F32)]
    wide, column = shape(rows, cols), shape(rows, 128, F32)
    chip_u, cross_u, norm, grad, value = call(
        part(meet_own, share), [wide, wide, column, *sums], whole, core, near01, far, half, rest
    )
    points_of = (whole, core, chip_u, cross_u)
    grad, value = call(part(meet_next, share), sums, *points_of, norm, next01, next23, grad, value)
    grad, value = call(part(meet_across, share), sums, *points_of, norm, across, grad, value)
    table = shape(rows, share)
    send, kern, minus, total, lines = call(
        part(meet_last, share),
        [shape(rows + 16, cols), table, table, column, shape(16, 128, F32)],
        *points_of,
        norm,
        last01,
        last23,
        grad,
        value,
    )
    back = permute(send, 0, 1)
    weights = (kern, minus, total)
    keep_chip = call(
        part(finish_chip, share), [shape(rows, cols, F32)], chip_u, *weights, last23, grad
    )[0]
    send, lines = call(
        part(sum_cores, rows), [shape(rows + 16, cols), shape(16, 128, F32)], keep_chip, lines, back
    )
    far = permute(send, 0, 2)
    send = call(part(finish_core, share), [wide], core, *weights, last01, grad)[0]
    back = permute(send, 0, 1)
    keep = call(
        part(finish_own, share), [shape(rows, cols, F32)], whole, *weights, last01, grad
    )[0]
    grad, value = call(
        part(sum_chips, rows), [shape(rows, cols, F32), shape(rows // 128, 128, F32)], keep, back, far, lines
    )
    return value.reshape(rows), grad


def solution(mesh):
    return jax.shard_map(
        body,
        mesh=mesh,
        in_specs=(P("pts", "dim"), P("pts", "dim"), P("pts")),
        out_specs=(P("pts"), P("pts", "dim")),
        check_vma=False,
    )
```

```python
import functools

import jax
import jax.numpy as jnp
from jax import lax
from jax.experimental import pallas as pl
from jax.experimental.pallas import tpu as pltpu
from jax.sharding import PartitionSpec as P

F32, BF16 = jnp.float32, jnp.bfloat16
VMEM = pl.BlockSpec(memory_space=pltpu.VMEM)
ANY = pl.BlockSpec(memory_space=pltpu.HBM)
NT = (((1,), (1,)), ((), ()))
SPACING = 2_000_000_000


def permute(array, pts, dim):
    devices_p, devices_d = lax.axis_size("pts"), lax.axis_size("dim")
    pairs = [
        (p * devices_d + d, (p ^ pts) * devices_d + (d ^ dim))
        for p in range(devices_p)
        for d in range(devices_d)
    ]
    return lax.ppermute(array, ("pts", "dim"), pairs)


def call(kernel, outs, *args, flops=0, scratch=(), spec=VMEM):
    return pl.pallas_call(
        kernel,
        out_shape=outs,
        in_specs=[spec] * len(args),
        out_specs=[VMEM] * len(outs),
        scratch_shapes=scratch,
        compiler_params=pltpu.CompilerParams(vmem_limit_bytes=16 << 20),
        cost_estimate=pl.CostEstimate(flops=flops, bytes_accessed=0, transcendentals=0),
    )(*args)


def shape(rows, cols, dtype=BF16):
    return jax.ShapeDtypeStruct((rows, cols), dtype)


def quarter(which, size):
    return pl.ds(pl.multiple_of(which * size, 16), size)


def pack(share, u, b, whole, chip, cross, own, sems):
    rows, me = u.shape[0], lax.axis_index("dim")
    upper = pl.ds(0, share)
    lower = pl.ds(share, share)
    moves = [(u, whole.at[pl.ds(0, rows)]), (b.at[quarter(me ^ 1, share)], whole.at[pl.ds(rows, share)])]
    for which, out in ((2, chip), (3, cross), (0, own)):
        moves.append((u.at[quarter(me ^ which, share)], out.at[upper]))
        moves.append((b.at[quarter(me ^ which, share)], out.at[lower]))
    copies = [pltpu.make_async_copy(*move, sems.at[n]) for n, move in enumerate(moves)]
    for copy in copies:
        copy.start()
    for copy in copies:
        copy.wait()


def lay_near(share, own, core, near):
    rows, me = core.shape[0] - share, lax.axis_index("dim")
    near[: 2 * share] = own[...]
    near[2 * share : 3 * share] = core[quarter(me, share), :]
    near[3 * share :] = core[rows:]


def lay_far(share, chip, cross, coef, after, far):
    far[: 2 * share] = chip[...]
    far[2 * share : 4 * share] = cross[...]
    me, lanes = lax.axis_index("dim"), coef.shape[1]
    row = lax.broadcasted_iota(jnp.int32, coef.shape, 0)
    first, skip = me * share // lanes, me * share % lanes
    parts = [
        jnp.sum(jnp.where(row == first + n, coef[...], 0.0), 0, keepdims=True) for n in range(2)
    ]
    mine = jnp.broadcast_to(jnp.concatenate(parts, 1), (16, 2 * lanes))
    far[4 * share :] = pltpu.roll(mine, lax.rem(2 * lanes - skip, 2 * lanes), 1).astype(BF16)


def lay_across(far, after, out):
    out[...] = far[...]


def lay_half(share, whole, *refs):
    half = refs[-1]
    half[...] = whole[quarter(lax.axis_index("dim") // 2, 2 * share), :]


def lay_rest(share, far, half, rest):
    rest[:share] = far[:share]
    rest[share : 2 * share] = far[2 * share : 3 * share]
    rest[2 * share :] = half[...]


def as_row(column):
    size = column.shape[0]
    diagonal = lax.broadcasted_iota(jnp.int32, (size, size), 0) == lax.broadcasted_iota(
        jnp.int32, (size, size), 1
    )
    return jnp.sum(jnp.where(diagonal, column, 0.0), 0, keepdims=True)


def norms_of(slices):
    total = 0.0
    for part in slices:
        wide = part.astype(F32)
        total = total + wide * wide
    return jnp.sum(total, 1, keepdims=True)


def halves(share, ref):
    return ref.at[: 2 * share], ref.at[2 * share : 4 * share]


def dots(share, own, pieces):
    gram = cross = square = inner = 0.0
    for mine, piece in zip(own, pieces):
        far_u, far_b = piece[:share], piece[share : 2 * share]
        gram = gram + lax.dot_general(mine[...], far_u, NT, preferred_element_type=F32)
        cross = cross + lax.dot_general(mine[...], far_b, NT, preferred_element_type=F32)
        far_u = far_u.astype(F32)
        square = square + far_u * far_u
        inner = inner + far_u * far_b.astype(F32)
    return gram, cross, square, inner


def weigh(share, own_norm, gram, cross, square, inner, coef):
    norm = as_row(jnp.sum(square, 1, keepdims=True))
    inner = as_row(jnp.sum(inner, 1, keepdims=True))
    coef = coef[4 * share :].astype(F32)[:1, :share]
    kern = jnp.exp(gram - 0.5 * (own_norm + norm))
    return kern, kern * (coef + cross - inner)


def meet(share, own, own_norm, pieces, coef):
    return weigh(share, own_norm, *dots(share, own, pieces), coef)


def contribution(share, own, kern_b, minus_b, value, piece):
    return (
        jnp.dot(minus_b, piece[:share], preferred_element_type=F32)
        + jnp.dot(kern_b, piece[share : 2 * share], preferred_element_type=F32)
        - own[...].astype(F32) * value
    )


def meet_own(share, *refs):
    whole, core, near, far, half, rest, after, chip_u, cross_u, norm, grad, value = refs
    rows, me = whole.shape[0] - share, lax.axis_index("dim")
    other = quarter(1 - me // 2, 2 * share)
    chip, cross = halves(share, far)
    chip_u[quarter(me, share), :] = chip[:share]
    chip_u[quarter(me ^ 1, share), :] = rest[share : 2 * share]
    chip_u[other, :] = half[...]
    cross_u[quarter(me, share), :] = cross[:share]
    cross_u[quarter(me ^ 1, share), :] = rest[:share]
    cross_u[other, :] = rest[2 * share :]
    own = [whole[:rows], core[:rows], chip_u[...], cross_u[...]]
    own_norm = norms_of(own)
    norm[...] = jnp.broadcast_to(own_norm, norm.shape)
    pieces = [*halves(share, near), *halves(share, far)]
    kern, minus = meet(share, own, own_norm, pieces, far)
    total = jnp.sum(minus, 1, keepdims=True)
    value[...] = jnp.broadcast_to(total, value.shape)
    kern_b, minus_b = kern.astype(BF16), minus.astype(BF16)
    for k in range(4):
        grad[k * rows : (k + 1) * rows] = contribution(share, own[k], kern_b, minus_b, total, pieces[k])


def add_block(share, own, norm, pieces, coef, grad_in, value_in, grad, value):
    rows = norm.shape[0]
    kern, minus = meet(share, own, norm[:, :1], pieces, coef)
    total = jnp.sum(minus, 1, keepdims=True)
    value[...] = value_in[...] + total
    kern_b, minus_b = kern.astype(BF16), minus.astype(BF16)
    for k in range(4):
        at = slice(k * rows, (k + 1) * rows)
        grad[at] = grad_in[at] + contribution(share, own[k], kern_b, minus_b, total, pieces[k])


def meet_next(share, whole, core, chip_u, cross_u, norm, p01, p23, grad_in, value_in, grad, value):
    rows = norm.shape[0]
    own = [whole[:rows], core[:rows], chip_u[...], cross_u[...]]
    add_block(share, own, norm, [*halves(share, p01), *halves(share, p23)], p23, grad_in, value_in, grad, value)


def meet_across(share, *refs):
    whole, core, chip_u, cross_u, norm, p01, p23, grad_in, value_in, grad, value = refs
    rows = norm.shape[0]
    own = [whole[:rows], core[:rows], chip_u[...], cross_u[...]]
    pieces = [*halves(share, p23), *halves(share, p01)]
    add_block(share, own, norm, pieces, p23, grad_in, value_in, grad, value)


def put_values(out, start, rows_of):
    high = rows_of.astype(BF16)
    low = (rows_of - high.astype(F32)).astype(BF16)
    out[start:] = jnp.concatenate([high, low], 1)


def take_values(ref, start):
    both = ref[start:].astype(F32)
    half = both.shape[1] // 2
    return both[:, :half] + both[:, half:]


def begin_last(share, whole, core, p01, *outs):
    rows = whole.shape[0] - share
    for out, value in zip(outs, dots(share, [whole[:rows], core[:rows]], halves(share, p01))):
        out[...] = value


def meet_last(share, *refs):
    chip_u, cross_u, norm, p23, begun, grad, value_in, send, kern_b, minus_b, total, lines = (
        *refs[:4], refs[4:8], *refs[8:]
    )
    rows = chip_u.shape[0]
    p2, p3 = halves(share, p23)
    sums = [one[...] + more for one, more in zip(begun, dots(share, [chip_u, cross_u], [p2, p3]))]
    kern, minus = weigh(share, norm[:, :1], *sums, p23)
    part = jnp.sum(minus, 1, keepdims=True)
    kern_b[...] = kern.astype(BF16)
    minus_b[...] = minus.astype(BF16)
    total[...] = jnp.broadcast_to(part, total.shape)
    term = contribution(share, cross_u, kern_b[...], minus_b[...], part, p3)
    send[:rows] = (grad[3 * rows :] + term).astype(BF16)
    value = value_in[:, :1] + part
    rows_of = [as_row(value[at : at + 128]) for at in range(0, rows, 128)]
    rows_of += [jnp.zeros_like(rows_of[0])] * (16 - len(rows_of))
    lines[...] = jnp.concatenate(rows_of, 0)
    put_values(send, rows, lines[...])


def finish_chip(share, chip_u, kern_b, minus_b, total, p23, grad, out):
    rows = chip_u.shape[0]
    term = contribution(share, chip_u, kern_b[...], minus_b[...], total[:, :1], halves(share, p23)[0])
    out[...] = grad[2 * rows : 3 * rows] + term


def finish_core(share, core, kern_b, minus_b, total, p01, grad, send):
    rows = core.shape[0] - share
    term = contribution(share, core.at[:rows], kern_b[...], minus_b[...], total[:, :1], halves(share, p01)[1])
    send[...] = (grad[rows : 2 * rows] + term).astype(BF16)


def finish_own(share, whole, kern_b, minus_b, total, p01, grad, out):
    rows = whole.shape[0] - share
    term = contribution(share, whole.at[:rows], kern_b[...], minus_b[...], total[:, :1], halves(share, p01)[0])
    out[...] = grad[:rows] + term


def sum_cores(rows, keep, lines, back, send, both):
    send[:rows] = (keep[...] + back[:rows].astype(F32)).astype(BF16)
    both[...] = lines[...] + take_values(back, rows)
    put_values(send, rows, both[...])


def sum_chips(rows, keep, back, far, both, grad, value):
    grad[...] = keep[...] + back[...].astype(F32) + far[:rows].astype(F32)
    total = both[...] + take_values(far, rows)
    value[...] = total[: value.shape[0]]


def body(points, grad_weights, value_weights):
    rows, cols = points.shape
    share = rows // lax.axis_size("dim")
    piece = shape(2 * share, cols)
    part = functools.partial
    coef = value_weights.astype(F32).reshape(rows // 128, 128)

    whole, chip, cross, p0 = call(
        part(pack, share),
        [shape(rows + share, cols), piece, piece, piece],
        pltpu.with_memory_space_constraint(points, pltpu.HBM),
        pltpu.with_memory_space_constraint(grad_weights, pltpu.HBM),
        scratch=[pltpu.SemaphoreType.DMA((8,))],
        spec=ANY,
    )
    core = permute(whole, 0, 1)
    p2 = permute(chip, 0, 2)
    p3 = permute(cross, 0, 3)
    near = call(part(lay_near, share), [shape(4 * share, cols)], p0, core)[0]
    next01 = permute(near, 1, 0)
    across01 = permute(near, 4, 2)
    far = call(part(lay_far, share), [shape(4 * share + 16, cols)], p2, p3, coef, near)[0]
    next23 = permute(far, 1, 0)
    half = permute(call(part(lay_half, share), [piece], whole, far)[0], 0, 2)
    last01 = permute(next01, 3, 0)
    across23 = permute(call(lay_across, [shape(4 * share + 16, cols)], far, across01, flops=SPACING)[0], 4, 2)
    rest = call(part(lay_rest, share), [shape(4 * share, cols)], far, half)[0]
    rest = permute(rest, 0, 1)
    last23 = permute(next23, 3, 0)

    begun = call(
        part(begin_last, share),
        [*[shape(rows, share, F32)] * 2, *[shape(share, cols, F32)] * 2],
        whole,
        core,
        last01,
        flops=SPACING,
    )
    sums = [shape(4 * rows, cols, F32), shape(rows, 128, F32)]
    wide, column = shape(rows, cols), shape(rows, 128, F32)
    chip_u, cross_u, norm, grad, value = call(
        part(meet_own, share), [wide, wide, column, *sums], whole, core, near, far, half, rest, begun[0]
    )
    points_of = (whole, core, chip_u, cross_u)
    grad, value = call(part(meet_next, share), sums, *points_of, norm, next01, next23, grad, value)
    grad, value = call(part(meet_across, share), sums, *points_of, norm, across01, across23, grad, value)
    table = shape(rows, share)
    send, kern, minus, total, lines = call(
        part(meet_last, share),
        [shape(rows + 16, cols), table, table, column, shape(16, 128, F32)],
        chip_u,
        cross_u,
        norm,
        last23,
        *begun,
        grad,
        value,
    )
    back = permute(send, 0, 1)
    weights = (kern, minus, total)
    keep_chip = call(
        part(finish_chip, share), [shape(rows, cols, F32)], chip_u, *weights, last23, grad
    )[0]
    send, lines = call(
        part(sum_cores, rows), [shape(rows + 16, cols), shape(16, 128, F32)], keep_chip, lines, back
    )
    far = permute(send, 0, 2)
    send = call(part(finish_core, share), [wide], core, *weights, last01, grad)[0]
    back = permute(send, 0, 1)
    keep = call(
        part(finish_own, share), [shape(rows, cols, F32)], whole, *weights, last01, grad
    )[0]
    grad, value = call(
        part(sum_chips, rows), [shape(rows, cols, F32), shape(rows // 128, 128, F32)], keep, back, far, lines
    )
    return value.reshape(rows), grad


def solution(mesh):
    return jax.shard_map(
        body,
        mesh=mesh,
        in_specs=(P("pts", "dim"), P("pts", "dim"), P("pts")),
        out_specs=(P("pts"), P("pts", "dim")),
        check_vma=False,
    )
```

```python
import functools

import jax
import jax.numpy as jnp
from jax import lax
from jax.experimental import pallas as pl
from jax.experimental.pallas import tpu as pltpu
from jax.sharding import PartitionSpec as P

F32, BF16 = jnp.float32, jnp.bfloat16
VMEM = pl.BlockSpec(memory_space=pltpu.VMEM)
ANY = pl.BlockSpec(memory_space=pltpu.HBM)
NT = (((1,), (1,)), ((), ()))
SPACING = 2_000_000_000


def permute(array, pts, dim):
    devices_p, devices_d = lax.axis_size("pts"), lax.axis_size("dim")
    pairs = [
        (p * devices_d + d, (p ^ pts) * devices_d + (d ^ dim))
        for p in range(devices_p)
        for d in range(devices_d)
    ]
    return lax.ppermute(array, ("pts", "dim"), pairs)


def call(kernel, outs, *args, flops=0, scratch=(), spec=VMEM):
    return pl.pallas_call(
        kernel,
        out_shape=outs,
        in_specs=[spec] * len(args),
        out_specs=[VMEM] * len(outs),
        scratch_shapes=scratch,
        compiler_params=pltpu.CompilerParams(vmem_limit_bytes=16 << 20),
        cost_estimate=pl.CostEstimate(flops=flops, bytes_accessed=0, transcendentals=0),
    )(*args)


def shape(rows, cols, dtype=BF16):
    return jax.ShapeDtypeStruct((rows, cols), dtype)


def quarter(which, size):
    return pl.ds(pl.multiple_of(which * size, 16), size)


def pack(share, u, b, whole, chip, cross, own, sems):
    rows, me = u.shape[0], lax.axis_index("dim")
    upper = pl.ds(0, share)
    lower = pl.ds(share, share)
    moves = [(u, whole.at[pl.ds(0, rows)]), (b.at[quarter(me ^ 1, share)], whole.at[pl.ds(rows, share)])]
    for which, out in ((2, chip), (3, cross), (0, own)):
        moves.append((u.at[quarter(me ^ which, share)], out.at[upper]))
        moves.append((b.at[quarter(me ^ which, share)], out.at[lower]))
    copies = [pltpu.make_async_copy(*move, sems.at[n]) for n, move in enumerate(moves)]
    for copy in copies:
        copy.start()
    for copy in copies:
        copy.wait()


def lay_near(share, own, core, near):
    rows, me = core.shape[0] - share, lax.axis_index("dim")
    near[: 2 * share] = own[...]
    near[2 * share : 3 * share] = core[quarter(me, share), :]
    near[3 * share :] = core[rows:]


def lay_marked(share, cross, coef, after, piece):
    piece[: 2 * share] = cross[...]
    me, lanes = lax.axis_index("dim"), coef.shape[1]
    row = lax.broadcasted_iota(jnp.int32, coef.shape, 0)
    first, skip = me * share // lanes, me * share % lanes
    parts = [
        jnp.sum(jnp.where(row == first + n, coef[...], 0.0), 0, keepdims=True) for n in range(2)
    ]
    mine = jnp.broadcast_to(jnp.concatenate(parts, 1), (16, 2 * lanes))
    piece[2 * share :] = pltpu.roll(mine, lax.rem(2 * lanes - skip, 2 * lanes), 1).astype(BF16)


def lay_second(chip, *refs):
    refs[-1][...] = chip[...]


def lay_far(share, p2, p3, after, far):
    far[: 2 * share] = p2[...]
    far[2 * share :] = p3[...]


def lay_half(share, whole, *refs):
    half = refs[-1]
    half[...] = whole[quarter(lax.axis_index("dim") // 2, 2 * share), :]


def lay_rest(share, p2, p3, half, rest):
    rest[:share] = p2[:share]
    rest[share : 2 * share] = p3[:share]
    rest[2 * share :] = half[...]


def as_row(column):
    size = column.shape[0]
    diagonal = lax.broadcasted_iota(jnp.int32, (size, size), 0) == lax.broadcasted_iota(
        jnp.int32, (size, size), 1
    )
    return jnp.sum(jnp.where(diagonal, column, 0.0), 0, keepdims=True)


def norms_of(slices):
    total = 0.0
    for part in slices:
        wide = part.astype(F32)
        total = total + wide * wide
    return jnp.sum(total, 1, keepdims=True)


def halves(share, ref):
    return ref.at[: 2 * share], ref.at[2 * share : 4 * share]


def dots(share, own, pieces):
    gram = cross = square = inner = 0.0
    for mine, piece in zip(own, pieces):
        far_u, far_b = piece[:share], piece[share : 2 * share]
        gram = gram + lax.dot_general(mine[...], far_u, NT, preferred_element_type=F32)
        cross = cross + lax.dot_general(mine[...], far_b, NT, preferred_element_type=F32)
        far_u = far_u.astype(F32)
        square = square + far_u * far_u
        inner = inner + far_u * far_b.astype(F32)
    return gram, cross, square, inner


def weigh(share, own_norm, gram, cross, square, inner, coef):
    norm = as_row(jnp.sum(square, 1, keepdims=True))
    inner = as_row(jnp.sum(inner, 1, keepdims=True))
    coef = coef[2 * share :].astype(F32)[:1, :share]
    kern = jnp.exp(gram - 0.5 * (own_norm + norm))
    return kern, kern * (coef + cross - inner)


def meet(share, own, own_norm, pieces, coef):
    return weigh(share, own_norm, *dots(share, own, pieces), coef)


def contribution(share, own, kern_b, minus_b, value, piece):
    return (
        jnp.dot(minus_b, piece[:share], preferred_element_type=F32)
        + jnp.dot(kern_b, piece[share : 2 * share], preferred_element_type=F32)
        - own[...].astype(F32) * value
    )


def meet_own(share, *refs):
    whole, core, near, chip, cross, half, rest, after, chip_u, cross_u, norm, grad, value = refs
    rows, me = whole.shape[0] - share, lax.axis_index("dim")
    other = quarter(1 - me // 2, 2 * share)
    chip_u[quarter(me, share), :] = chip[:share]
    chip_u[quarter(me ^ 1, share), :] = rest[share : 2 * share]
    chip_u[other, :] = half[...]
    cross_u[quarter(me, share), :] = cross[:share]
    cross_u[quarter(me ^ 1, share), :] = rest[:share]
    cross_u[other, :] = rest[2 * share :]
    own = [whole[:rows], core[:rows], chip_u[...], cross_u[...]]
    own_norm = norms_of(own)
    norm[...] = jnp.broadcast_to(own_norm, norm.shape)
    pieces = [*halves(share, near), chip, cross]
    kern, minus = meet(share, own, own_norm, pieces, cross)
    total = jnp.sum(minus, 1, keepdims=True)
    value[...] = jnp.broadcast_to(total, value.shape)
    kern_b, minus_b = kern.astype(BF16), minus.astype(BF16)
    for k in range(4):
        grad[k * rows : (k + 1) * rows] = contribution(share, own[k], kern_b, minus_b, total, pieces[k])


def add_block(share, own, norm, pieces, coef, grad_in, value_in, grad, value):
    rows = norm.shape[0]
    kern, minus = meet(share, own, norm[:, :1], pieces, coef)
    total = jnp.sum(minus, 1, keepdims=True)
    value[...] = value_in[...] + total
    kern_b, minus_b = kern.astype(BF16), minus.astype(BF16)
    for k in range(4):
        at = slice(k * rows, (k + 1) * rows)
        grad[at] = grad_in[at] + contribution(share, own[k], kern_b, minus_b, total, pieces[k])


def meet_next(share, whole, core, chip_u, cross_u, norm, p01, p2, p3, grad_in, value_in, grad, value):
    rows = norm.shape[0]
    own = [whole[:rows], core[:rows], chip_u[...], cross_u[...]]
    add_block(share, own, norm, [*halves(share, p01), p2, p3], p3, grad_in, value_in, grad, value)


def meet_across(share, *refs):
    whole, core, chip_u, cross_u, norm, p01, p23, grad_in, value_in, grad, value = refs
    rows = norm.shape[0]
    own = [whole[:rows], core[:rows], chip_u[...], cross_u[...]]
    pieces = [*halves(share, p23), *halves(share, p01)]
    add_block(share, own, norm, pieces, p23.at[2 * share :], grad_in, value_in, grad, value)


def put_values(out, start, rows_of):
    high = rows_of.astype(BF16)
    low = (rows_of - high.astype(F32)).astype(BF16)
    out[start:] = jnp.concatenate([high, low], 1)


def take_values(ref, start):
    both = ref[start:].astype(F32)
    half = both.shape[1] // 2
    return both[:, :half] + both[:, half:]


def begin_last(share, whole, core, p01, *outs):
    rows = whole.shape[0] - share
    for out, value in zip(outs, dots(share, [whole[:rows], core[:rows]], halves(share, p01))):
        out[...] = value


def meet_last(share, *refs):
    chip_u, cross_u, norm, p2, p3, begun, grad, value_in, send, kern_b, minus_b, total, lines = (
        *refs[:5], refs[5:9], *refs[9:]
    )
    rows = chip_u.shape[0]
    sums = [one[...] + more for one, more in zip(begun, dots(share, [chip_u, cross_u], [p2, p3]))]
    kern, minus = weigh(share, norm[:, :1], *sums, p3)
    part = jnp.sum(minus, 1, keepdims=True)
    kern_b[...] = kern.astype(BF16)
    minus_b[...] = minus.astype(BF16)
    total[...] = jnp.broadcast_to(part, total.shape)
    term = contribution(share, cross_u, kern_b[...], minus_b[...], part, p3)
    send[:rows] = (grad[3 * rows :] + term).astype(BF16)
    value = value_in[:, :1] + part
    rows_of = [as_row(value[at : at + 128]) for at in range(0, rows, 128)]
    rows_of += [jnp.zeros_like(rows_of[0])] * (16 - len(rows_of))
    lines[...] = jnp.concatenate(rows_of, 0)
    put_values(send, rows, lines[...])


def finish_chip(share, chip_u, kern_b, minus_b, total, p2, grad, out):
    rows = chip_u.shape[0]
    term = contribution(share, chip_u, kern_b[...], minus_b[...], total[:, :1], p2)
    out[...] = grad[2 * rows : 3 * rows] + term


def finish_core(share, core, kern_b, minus_b, total, p01, grad, send):
    rows = core.shape[0] - share
    term = contribution(share, core.at[:rows], kern_b[...], minus_b[...], total[:, :1], halves(share, p01)[1])
    send[...] = (grad[rows : 2 * rows] + term).astype(BF16)


def finish_own(share, whole, kern_b, minus_b, total, p01, grad, out):
    rows = whole.shape[0] - share
    term = contribution(share, whole.at[:rows], kern_b[...], minus_b[...], total[:, :1], halves(share, p01)[0])
    out[...] = grad[:rows] + term


def sum_cores(rows, keep, lines, back, send, both):
    send[:rows] = (keep[...] + back[:rows].astype(F32)).astype(BF16)
    both[...] = lines[...] + take_values(back, rows)
    put_values(send, rows, both[...])


def sum_chips(rows, keep, back, far, both, grad, value):
    grad[...] = keep[...] + back[...].astype(F32) + far[:rows].astype(F32)
    total = both[...] + take_values(far, rows)
    value[...] = total[: value.shape[0]]


def body(points, grad_weights, value_weights):
    rows, cols = points.shape
    share = rows // lax.axis_size("dim")
    piece = shape(2 * share, cols)
    part = functools.partial
    coef = value_weights.astype(F32).reshape(rows // 128, 128)

    whole, chip, cross, p0 = call(
        part(pack, share),
        [shape(rows + share, cols), piece, piece, piece],
        pltpu.with_memory_space_constraint(points, pltpu.HBM),
        pltpu.with_memory_space_constraint(grad_weights, pltpu.HBM),
        scratch=[pltpu.SemaphoreType.DMA((8,))],
        spec=ANY,
    )
    core = permute(whole, 0, 1)
    p2 = permute(chip, 0, 2)
    p3 = permute(cross, 0, 3)
    near = call(part(lay_near, share), [shape(4 * share, cols)], p0, core)[0]
    next01 = permute(near, 1, 0)
    across01 = permute(near, 4, 2)
    p3 = call(part(lay_marked, share), [shape(2 * share + 16, cols)], p3, coef, near)[0]
    p2 = call(lay_second, [piece], p2, near, flops=SPACING)[0]
    next2, next3 = permute(p2, 1, 0), permute(p3, 1, 0)
    half = permute(call(part(lay_half, share), [piece], whole, p3)[0], 0, 2)
    last01 = permute(next01, 3, 0)
    far = call(part(lay_far, share), [shape(4 * share + 16, cols)], p2, p3, across01, flops=SPACING)[0]
    across23 = permute(far, 4, 2)
    last2 = permute(next2, 3, 0)
    rest = call(part(lay_rest, share), [shape(4 * share, cols)], p2, p3, half)[0]
    rest = permute(rest, 0, 1)
    last3 = permute(next3, 3, 0)

    begun = call(
        part(begin_last, share),
        [*[shape(rows, share, F32)] * 2, *[shape(share, cols, F32)] * 2],
        whole,
        core,
        last01,
        flops=SPACING,
    )
    sums = [shape(4 * rows, cols, F32), shape(rows, 128, F32)]
    wide, column = shape(rows, cols), shape(rows, 128, F32)
    chip_u, cross_u, norm, grad, value = call(
        part(meet_own, share), [wide, wide, column, *sums], whole, core, near, p2, p3, half, rest, begun[0]
    )
    points_of = (whole, core, chip_u, cross_u)
    grad, value = call(part(meet_next, share), sums, *points_of, norm, next01, next2, next3, grad, value)
    grad, value = call(part(meet_across, share), sums, *points_of, norm, across01, across23, grad, value)
    table = shape(rows, share)
    send, kern, minus, total, lines = call(
        part(meet_last, share),
        [shape(rows + 16, cols), table, table, column, shape(16, 128, F32)],
        chip_u,
        cross_u,
        norm,
        last2,
        last3,
        *begun,
        grad,
        value,
    )
    back = permute(send, 0, 1)
    weights = (kern, minus, total)
    keep_chip = call(
        part(finish_chip, share), [shape(rows, cols, F32)], chip_u, *weights, last2, grad
    )[0]
    send, lines = call(
        part(sum_cores, rows), [shape(rows + 16, cols), shape(16, 128, F32)], keep_chip, lines, back
    )
    far = permute(send, 0, 2)
    send = call(part(finish_core, share), [wide], core, *weights, last01, grad)[0]
    back = permute(send, 0, 1)
    keep = call(
        part(finish_own, share), [shape(rows, cols, F32)], whole, *weights, last01, grad
    )[0]
    grad, value = call(
        part(sum_chips, rows), [shape(rows, cols, F32), shape(rows // 128, 128, F32)], keep, back, far, lines
    )
    return value.reshape(rows), grad


def solution(mesh):
    return jax.shard_map(
        body,
        mesh=mesh,
        in_specs=(P("pts", "dim"), P("pts", "dim"), P("pts")),
        out_specs=(P("pts"), P("pts", "dim")),
        check_vma=False,
    )
```

```python
import functools

import jax
import jax.numpy as jnp
from jax import lax
from jax.experimental import pallas as pl
from jax.experimental.pallas import tpu as pltpu
from jax.sharding import PartitionSpec as P

F32, BF16 = jnp.float32, jnp.bfloat16
VMEM = pl.BlockSpec(memory_space=pltpu.VMEM)
ANY = pl.BlockSpec(memory_space=pltpu.HBM)
NT = (((1,), (1,)), ((), ()))
SPACING = 2_000_000_000


def permute(array, pts, dim):
    devices_p, devices_d = lax.axis_size("pts"), lax.axis_size("dim")
    pairs = [
        (p * devices_d + d, (p ^ pts) * devices_d + (d ^ dim))
        for p in range(devices_p)
        for d in range(devices_d)
    ]
    return lax.ppermute(array, ("pts", "dim"), pairs)


def call(kernel, outs, *args, flops=0, scratch=(), spec=VMEM):
    return pl.pallas_call(
        kernel,
        out_shape=outs,
        in_specs=[spec] * len(args),
        out_specs=[VMEM] * len(outs),
        scratch_shapes=scratch,
        compiler_params=pltpu.CompilerParams(vmem_limit_bytes=16 << 20),
        cost_estimate=pl.CostEstimate(flops=flops, bytes_accessed=0, transcendentals=0),
    )(*args)


def shape(rows, cols, dtype=BF16):
    return jax.ShapeDtypeStruct((rows, cols), dtype)


def quarter(which, size):
    return pl.ds(pl.multiple_of(which * size, 16), size)


def pack(share, u, b, whole, chip, cross, own, sems):
    rows, me = u.shape[0], lax.axis_index("dim")
    upper = pl.ds(0, share)
    lower = pl.ds(share, share)
    moves = [(u, whole.at[pl.ds(0, rows)]), (b.at[quarter(me ^ 1, share)], whole.at[pl.ds(rows, share)])]
    for which, out in ((2, chip), (3, cross), (0, own)):
        moves.append((u.at[quarter(me ^ which, share)], out.at[upper]))
        moves.append((b.at[quarter(me ^ which, share)], out.at[lower]))
    copies = [pltpu.make_async_copy(*move, sems.at[n]) for n, move in enumerate(moves)]
    for copy in copies:
        copy.start()
    for copy in copies:
        copy.wait()


def lay_near(share, own, core, near):
    rows, me = core.shape[0] - share, lax.axis_index("dim")
    near[: 2 * share] = own[...]
    near[2 * share : 3 * share] = core[quarter(me, share), :]
    near[3 * share :] = core[rows:]


def lay_marked(share, cross, coef, after, piece):
    piece[: 2 * share] = cross[...]
    me, lanes = lax.axis_index("dim"), coef.shape[1]
    row = lax.broadcasted_iota(jnp.int32, coef.shape, 0)
    first, skip = me * share // lanes, me * share % lanes
    parts = [
        jnp.sum(jnp.where(row == first + n, coef[...], 0.0), 0, keepdims=True) for n in range(2)
    ]
    mine = jnp.broadcast_to(jnp.concatenate(parts, 1), (16, 2 * lanes))
    piece[2 * share :] = pltpu.roll(mine, lax.rem(2 * lanes - skip, 2 * lanes), 1).astype(BF16)


def lay_second(chip, *refs):
    refs[-1][...] = chip[...]


def lay_far(share, p2, p3, after, far):
    far[: 2 * share] = p2[...]
    far[2 * share :] = p3[...]


def lay_half(share, whole, *refs):
    half = refs[-1]
    half[...] = whole[quarter(lax.axis_index("dim") // 2, 2 * share), :]


def lay_rest(share, p2, p3, half, rest):
    rest[:share] = p2[:share]
    rest[share : 2 * share] = p3[:share]
    rest[2 * share :] = half[...]


def as_row(column):
    size = column.shape[0]
    diagonal = lax.broadcasted_iota(jnp.int32, (size, size), 0) == lax.broadcasted_iota(
        jnp.int32, (size, size), 1
    )
    return jnp.sum(jnp.where(diagonal, column, 0.0), 0, keepdims=True)


def norms_of(slices):
    total = 0.0
    for part in slices:
        wide = part.astype(F32)
        total = total + wide * wide
    return jnp.sum(total, 1, keepdims=True)


def halves(share, ref):
    return ref.at[: 2 * share], ref.at[2 * share : 4 * share]


def dots(share, own, pieces):
    gram = cross = square = inner = 0.0
    for mine, piece in zip(own, pieces):
        far_u, far_b = piece[:share], piece[share : 2 * share]
        gram = gram + lax.dot_general(mine[...], far_u, NT, preferred_element_type=F32)
        cross = cross + lax.dot_general(mine[...], far_b, NT, preferred_element_type=F32)
        far_u = far_u.astype(F32)
        square = square + far_u * far_u
        inner = inner + far_u * far_b.astype(F32)
    return gram, cross, square, inner


def weigh(share, own_norm, gram, cross, square, inner, coef):
    norm = as_row(jnp.sum(square, 1, keepdims=True))
    inner = as_row(jnp.sum(inner, 1, keepdims=True))
    coef = coef[2 * share :].astype(F32)[:1, :share]
    kern = jnp.exp(gram - 0.5 * (own_norm + norm))
    return kern, kern * (coef + cross - inner)


def meet(share, own, own_norm, pieces, coef):
    return weigh(share, own_norm, *dots(share, own, pieces), coef)


def contribution(share, own, kern_b, minus_b, value, piece):
    return (
        jnp.dot(minus_b, piece[:share], preferred_element_type=F32)
        + jnp.dot(kern_b, piece[share : 2 * share], preferred_element_type=F32)
        - own[...].astype(F32) * value
    )


def meet_own(share, *refs):
    whole, core, near, chip, cross, half, rest, after, chip_u, cross_u, norm, grad, value = refs
    rows, me = whole.shape[0] - share, lax.axis_index("dim")
    other = quarter(1 - me // 2, 2 * share)
    chip_u[quarter(me, share), :] = chip[:share]
    chip_u[quarter(me ^ 1, share), :] = rest[share : 2 * share]
    chip_u[other, :] = half[...]
    cross_u[quarter(me, share), :] = cross[:share]
    cross_u[quarter(me ^ 1, share), :] = rest[:share]
    cross_u[other, :] = rest[2 * share :]
    own = [whole[:rows], core[:rows], chip_u[...], cross_u[...]]
    own_norm = norms_of(own)
    norm[...] = jnp.broadcast_to(own_norm, norm.shape)
    pieces = [*halves(share, near), chip, cross]
    kern, minus = meet(share, own, own_norm, pieces, cross)
    total = jnp.sum(minus, 1, keepdims=True)
    value[...] = jnp.broadcast_to(total, value.shape)
    kern_b, minus_b = kern.astype(BF16), minus.astype(BF16)
    for k in range(4):
        grad[k * rows : (k + 1) * rows] = contribution(share, own[k], kern_b, minus_b, total, pieces[k])


def add_block(share, own, norm, pieces, coef, grad_in, value_in, grad, value):
    rows = norm.shape[0]
    kern, minus = meet(share, own, norm[:, :1], pieces, coef)
    total = jnp.sum(minus, 1, keepdims=True)
    value[...] = value_in[...] + total
    kern_b, minus_b = kern.astype(BF16), minus.astype(BF16)
    for k in range(4):
        at = slice(k * rows, (k + 1) * rows)
        grad[at] = grad_in[at] + contribution(share, own[k], kern_b, minus_b, total, pieces[k])


def meet_next(share, whole, core, chip_u, cross_u, norm, p01, p2, p3, grad_in, value_in, grad, value):
    rows = norm.shape[0]
    own = [whole[:rows], core[:rows], chip_u[...], cross_u[...]]
    add_block(share, own, norm, [*halves(share, p01), p2, p3], p3, grad_in, value_in, grad, value)


def meet_across(share, *refs):
    whole, core, chip_u, cross_u, norm, p01, p23, grad_in, value_in, grad, value = refs
    rows = norm.shape[0]
    own = [whole[:rows], core[:rows], chip_u[...], cross_u[...]]
    pieces = [*halves(share, p23), *halves(share, p01)]
    add_block(share, own, norm, pieces, p23.at[2 * share :], grad_in, value_in, grad, value)


def put_values(out, start, rows_of):
    high = rows_of.astype(BF16)
    low = (rows_of - high.astype(F32)).astype(BF16)
    out[start:] = jnp.concatenate([high, low], 1)


def take_values(ref, start):
    both = ref[start:].astype(F32)
    half = both.shape[1] // 2
    return both[:, :half] + both[:, half:]


def begin_last(share, whole, core, p01, *outs):
    rows = whole.shape[0] - share
    for out, value in zip(outs, dots(share, [whole[:rows], core[:rows]], halves(share, p01))):
        out[...] = value


def meet_last(share, *refs):
    chip_u, cross_u, norm, p2, p3, begun, grad, value_in, send, kern_b, minus_b, total, lines = (
        *refs[:5], refs[5:9], *refs[9:]
    )
    rows = chip_u.shape[0]
    sums = [one[...] + more for one, more in zip(begun, dots(share, [chip_u, cross_u], [p2, p3]))]
    kern, minus = weigh(share, norm[:, :1], *sums, p3)
    part = jnp.sum(minus, 1, keepdims=True)
    kern_b[...] = kern.astype(BF16)
    minus_b[...] = minus.astype(BF16)
    total[...] = jnp.broadcast_to(part, total.shape)
    term = contribution(share, cross_u, kern_b[...], minus_b[...], part, p3)
    send[:rows] = (grad[3 * rows :] + term).astype(BF16)
    value = value_in[:, :1] + part
    rows_of = [as_row(value[at : at + 128]) for at in range(0, rows, 128)]
    rows_of += [jnp.zeros_like(rows_of[0])] * (16 - len(rows_of))
    lines[...] = jnp.concatenate(rows_of, 0)
    put_values(send, rows, lines[...])


def finish_chip(share, chip_u, kern_b, minus_b, total, p2, grad, out):
    rows = chip_u.shape[0]
    term = contribution(share, chip_u, kern_b[...], minus_b[...], total[:, :1], p2)
    out[...] = grad[2 * rows : 3 * rows] + term


def finish_core(share, core, kern_b, minus_b, total, p01, grad, send):
    rows = core.shape[0] - share
    term = contribution(share, core.at[:rows], kern_b[...], minus_b[...], total[:, :1], halves(share, p01)[1])
    send[...] = (grad[rows : 2 * rows] + term).astype(BF16)


def finish_own(share, whole, kern_b, minus_b, total, p01, grad, back, out):
    rows = whole.shape[0] - share
    term = contribution(share, whole.at[:rows], kern_b[...], minus_b[...], total[:, :1], halves(share, p01)[0])
    out[...] = grad[:rows] + term + back[...].astype(F32)


def sum_cores(rows, keep, lines, back, send, both):
    send[:rows] = (keep[...] + back[:rows].astype(F32)).astype(BF16)
    both[...] = lines[...] + take_values(back, rows)
    put_values(send, rows, both[...])


def sum_chips(rows, keep, far, both, grad, value):
    grad[...] = keep[...] + far[:rows].astype(F32)
    total = both[...] + take_values(far, rows)
    value[...] = total[: value.shape[0]]


def body(points, grad_weights, value_weights):
    rows, cols = points.shape
    share = rows // lax.axis_size("dim")
    piece = shape(2 * share, cols)
    part = functools.partial
    coef = value_weights.astype(F32).reshape(rows // 128, 128)

    whole, chip, cross, p0 = call(
        part(pack, share),
        [shape(rows + share, cols), piece, piece, piece],
        pltpu.with_memory_space_constraint(points, pltpu.HBM),
        pltpu.with_memory_space_constraint(grad_weights, pltpu.HBM),
        scratch=[pltpu.SemaphoreType.DMA((8,))],
        spec=ANY,
    )
    core = permute(whole, 0, 1)
    p2 = permute(chip, 0, 2)
    p3 = permute(cross, 0, 3)
    near = call(part(lay_near, share), [shape(4 * share, cols)], p0, core)[0]
    next01 = permute(near, 1, 0)
    across01 = permute(near, 4, 2)
    p3 = call(part(lay_marked, share), [shape(2 * share + 16, cols)], p3, coef, near)[0]
    p2 = call(lay_second, [piece], p2, near, flops=SPACING)[0]
    next2, next3 = permute(p2, 1, 0), permute(p3, 1, 0)
    half = permute(call(part(lay_half, share), [piece], whole, p3)[0], 0, 2)
    last01 = permute(next01, 3, 0)
    far = call(part(lay_far, share), [shape(4 * share + 16, cols)], p2, p3, across01, flops=SPACING)[0]
    across23 = permute(far, 4, 2)
    last2 = permute(next2, 3, 0)
    rest = call(part(lay_rest, share), [shape(4 * share, cols)], p2, p3, half)[0]
    rest = permute(rest, 0, 1)
    last3 = permute(next3, 3, 0)

    begun = call(
        part(begin_last, share),
        [*[shape(rows, share, F32)] * 2, *[shape(share, cols, F32)] * 2],
        whole,
        core,
        last01,
        flops=SPACING,
    )
    sums = [shape(4 * rows, cols, F32), shape(rows, 128, F32)]
    wide, column = shape(rows, cols), shape(rows, 128, F32)
    chip_u, cross_u, norm, grad, value = call(
        part(meet_own, share), [wide, wide, column, *sums], whole, core, near, p2, p3, half, rest, begun[0]
    )
    points_of = (whole, core, chip_u, cross_u)
    grad, value = call(part(meet_next, share), sums, *points_of, norm, next01, next2, next3, grad, value)
    grad, value = call(part(meet_across, share), sums, *points_of, norm, across01, across23, grad, value)
    table = shape(rows, share)
    send, kern, minus, total, lines = call(
        part(meet_last, share),
        [shape(rows + 16, cols), table, table, column, shape(16, 128, F32)],
        chip_u,
        cross_u,
        norm,
        last2,
        last3,
        *begun,
        grad,
        value,
    )
    back = permute(send, 0, 1)
    weights = (kern, minus, total)
    keep_chip = call(
        part(finish_chip, share), [shape(rows, cols, F32)], chip_u, *weights, last2, grad
    )[0]
    send, lines = call(
        part(sum_cores, rows), [shape(rows + 16, cols), shape(16, 128, F32)], keep_chip, lines, back
    )
    far = permute(send, 0, 2)
    send = call(part(finish_core, share), [wide], core, *weights, last01, grad)[0]
    back = permute(send, 0, 1)
    keep = call(
        part(finish_own, share), [shape(rows, cols, F32)], whole, *weights, last01, grad, back
    )[0]
    grad, value = call(
        part(sum_chips, rows), [shape(rows, cols, F32), shape(rows // 128, 128, F32)], keep, far, lines
    )
    return value.reshape(rows), grad


def solution(mesh):
    return jax.shard_map(
        body,
        mesh=mesh,
        in_specs=(P("pts", "dim"), P("pts", "dim"), P("pts")),
        out_specs=(P("pts"), P("pts", "dim")),
        check_vma=False,
    )
```

```python
import functools

import jax
import jax.numpy as jnp
from jax import lax
from jax.experimental import pallas as pl
from jax.experimental.pallas import tpu as pltpu
from jax.sharding import PartitionSpec as P

F32, BF16 = jnp.float32, jnp.bfloat16
VMEM = pl.BlockSpec(memory_space=pltpu.VMEM)
ANY = pl.BlockSpec(memory_space=pltpu.HBM)
NT = (((1,), (1,)), ((), ()))
SPACING = 2_000_000_000


def permute(array, pts, dim):
    devices_p, devices_d = lax.axis_size("pts"), lax.axis_size("dim")
    pairs = [
        (p * devices_d + d, (p ^ pts) * devices_d + (d ^ dim))
        for p in range(devices_p)
        for d in range(devices_d)
    ]
    return lax.ppermute(array, ("pts", "dim"), pairs)


def call(kernel, outs, *args, flops=0, scratch=(), spec=VMEM):
    return pl.pallas_call(
        kernel,
        out_shape=outs,
        in_specs=[spec] * len(args),
        out_specs=[VMEM] * len(outs),
        scratch_shapes=scratch,
        compiler_params=pltpu.CompilerParams(vmem_limit_bytes=16 << 20),
        cost_estimate=pl.CostEstimate(flops=flops, bytes_accessed=0, transcendentals=0),
    )(*args)


def shape(rows, cols, dtype=BF16):
    return jax.ShapeDtypeStruct((rows, cols), dtype)


def quarter(which, size):
    return pl.ds(pl.multiple_of(which * size, 16), size)


def pack(share, u, b, whole, chip, cross, own, sems):
    rows, me = u.shape[0], lax.axis_index("dim")
    upper = pl.ds(0, share)
    lower = pl.ds(share, share)
    moves = [(u, whole.at[pl.ds(0, rows)]), (b.at[quarter(me ^ 1, share)], whole.at[pl.ds(rows, share)])]
    for which, out in ((2, chip), (3, cross), (0, own)):
        moves.append((u.at[quarter(me ^ which, share)], out.at[upper]))
        moves.append((b.at[quarter(me ^ which, share)], out.at[lower]))
    copies = [pltpu.make_async_copy(*move, sems.at[n]) for n, move in enumerate(moves)]
    for copy in copies:
        copy.start()
    for copy in copies:
        copy.wait()


def lay_near(share, own, core, near):
    rows, me = core.shape[0] - share, lax.axis_index("dim")
    near[: 2 * share] = own[...]
    near[2 * share : 3 * share] = core[quarter(me, share), :]
    near[3 * share :] = core[rows:]


def lay_marked(share, cross, coef, after, piece):
    piece[: 2 * share] = cross[...]
    me, lanes = lax.axis_index("dim"), coef.shape[1]
    row = lax.broadcasted_iota(jnp.int32, coef.shape, 0)
    first, skip = me * share // lanes, me * share % lanes
    parts = [
        jnp.sum(jnp.where(row == first + n, coef[...], 0.0), 0, keepdims=True) for n in range(2)
    ]
    mine = jnp.broadcast_to(jnp.concatenate(parts, 1), (16, 2 * lanes))
    piece[2 * share :] = pltpu.roll(mine, lax.rem(2 * lanes - skip, 2 * lanes), 1).astype(BF16)


def lay_second(chip, *refs):
    refs[-1][...] = chip[...]


def lay_far(share, p2, p3, after, far):
    far[: 2 * share] = p2[...]
    far[2 * share :] = p3[...]


def lay_half(share, whole, *refs):
    half = refs[-1]
    half[...] = whole[quarter(lax.axis_index("dim") // 2, 2 * share), :]


def lay_rest(share, p2, p3, half, rest):
    rest[:share] = p2[:share]
    rest[share : 2 * share] = p3[:share]
    rest[2 * share :] = half[...]


def as_row(column):
    size = column.shape[0]
    diagonal = lax.broadcasted_iota(jnp.int32, (size, size), 0) == lax.broadcasted_iota(
        jnp.int32, (size, size), 1
    )
    return jnp.sum(jnp.where(diagonal, column, 0.0), 0, keepdims=True)


def norms_of(slices):
    total = 0.0
    for part in slices:
        wide = part.astype(F32)
        total = total + wide * wide
    return jnp.sum(total, 1, keepdims=True)


def halves(share, ref):
    return ref.at[: 2 * share], ref.at[2 * share : 4 * share]


def dots(share, own, pieces):
    gram = cross = square = inner = 0.0
    for mine, piece in zip(own, pieces):
        far_u, far_b = piece[:share], piece[share : 2 * share]
        gram = gram + lax.dot_general(mine[...], far_u, NT, preferred_element_type=F32)
        cross = cross + lax.dot_general(mine[...], far_b, NT, preferred_element_type=F32)
        far_u = far_u.astype(F32)
        square = square + far_u * far_u
        inner = inner + far_u * far_b.astype(F32)
    return gram, cross, square, inner


def weigh(share, own_norm, gram, cross, square, inner, coef):
    norm = as_row(jnp.sum(square, 1, keepdims=True))
    inner = as_row(jnp.sum(inner, 1, keepdims=True))
    coef = coef[2 * share :].astype(F32)[:1, :share]
    kern = jnp.exp(gram - 0.5 * (own_norm + norm))
    return kern, kern * (coef + cross - inner)


def meet(share, own, own_norm, pieces, coef):
    return weigh(share, own_norm, *dots(share, own, pieces), coef)


def contribution(share, own, kern_b, minus_b, value, piece):
    return (
        jnp.dot(minus_b, piece[:share], preferred_element_type=F32)
        + jnp.dot(kern_b, piece[share : 2 * share], preferred_element_type=F32)
        - own[...].astype(F32) * value
    )


def meet_own(share, *refs):
    whole, core, near, chip, cross, half, rest, after, chip_u, cross_u, norm, grad, value = refs
    rows, me = whole.shape[0] - share, lax.axis_index("dim")
    other = quarter(1 - me // 2, 2 * share)
    chip_u[quarter(me, share), :] = chip[:share]
    chip_u[quarter(me ^ 1, share), :] = rest[share : 2 * share]
    chip_u[other, :] = half[...]
    cross_u[quarter(me, share), :] = cross[:share]
    cross_u[quarter(me ^ 1, share), :] = rest[:share]
    cross_u[other, :] = rest[2 * share :]
    own = [whole[:rows], core[:rows], chip_u[...], cross_u[...]]
    own_norm = norms_of(own)
    norm[...] = jnp.broadcast_to(own_norm, norm.shape)
    pieces = [*halves(share, near), chip, cross]
    kern, minus = meet(share, own, own_norm, pieces, cross)
    total = jnp.sum(minus, 1, keepdims=True)
    value[...] = jnp.broadcast_to(total, value.shape)
    kern_b, minus_b = kern.astype(BF16), minus.astype(BF16)
    for k in range(4):
        grad[k * rows : (k + 1) * rows] = contribution(share, own[k], kern_b, minus_b, total, pieces[k])


def add_block(share, own, norm, pieces, coef, grad_in, value_in, grad, value):
    rows = norm.shape[0]
    kern, minus = meet(share, own, norm[:, :1], pieces, coef)
    total = jnp.sum(minus, 1, keepdims=True)
    value[...] = value_in[...] + total
    kern_b, minus_b = kern.astype(BF16), minus.astype(BF16)
    for k in range(4):
        at = slice(k * rows, (k + 1) * rows)
        grad[at] = grad_in[at] + contribution(share, own[k], kern_b, minus_b, total, pieces[k])


def meet_next(share, whole, core, chip_u, cross_u, norm, p01, p2, p3, grad_in, value_in, grad, value):
    rows = norm.shape[0]
    own = [whole[:rows], core[:rows], chip_u[...], cross_u[...]]
    add_block(share, own, norm, [*halves(share, p01), p2, p3], p3, grad_in, value_in, grad, value)


def meet_across(share, *refs):
    whole, core, chip_u, cross_u, norm, p01, p23, grad_in, value_in, grad, value = refs
    rows = norm.shape[0]
    own = [whole[:rows], core[:rows], chip_u[...], cross_u[...]]
    pieces = [*halves(share, p23), *halves(share, p01)]
    add_block(share, own, norm, pieces, p23.at[2 * share :], grad_in, value_in, grad, value)


def put_values(out, start, rows_of):
    high = rows_of.astype(BF16)
    low = (rows_of - high.astype(F32)).astype(BF16)
    out[start:] = jnp.concatenate([high, low], 1)


def take_values(ref, start):
    both = ref[start:].astype(F32)
    half = both.shape[1] // 2
    return both[:, :half] + both[:, half:]


def begin_last(share, whole, core, p01, *outs):
    rows = whole.shape[0] - share
    for out, value in zip(outs, dots(share, [whole[:rows], core[:rows]], halves(share, p01))):
        out[...] = value


def continue_last(share, chip_u, p2, *refs):
    more = dots(share, [chip_u], [p2])
    for out, before, value in zip(refs[4:], refs[:4], more):
        out[...] = before[...] + value


def meet_last(share, *refs):
    chip_u, cross_u, norm, p2, p3, begun, grad, value_in, send, kern_b, minus_b, total, lines = (
        *refs[:5], refs[5:9], *refs[9:]
    )
    rows = chip_u.shape[0]
    sums = [one[...] + more for one, more in zip(begun, dots(share, [cross_u], [p3]))]
    kern, minus = weigh(share, norm[:, :1], *sums, p3)
    part = jnp.sum(minus, 1, keepdims=True)
    kern_b[...] = kern.astype(BF16)
    minus_b[...] = minus.astype(BF16)
    total[...] = jnp.broadcast_to(part, total.shape)
    term = contribution(share, cross_u, kern_b[...], minus_b[...], part, p3)
    send[:rows] = (grad[3 * rows :] + term).astype(BF16)
    value = value_in[:, :1] + part
    rows_of = [as_row(value[at : at + 128]) for at in range(0, rows, 128)]
    rows_of += [jnp.zeros_like(rows_of[0])] * (16 - len(rows_of))
    lines[...] = jnp.concatenate(rows_of, 0)
    put_values(send, rows, lines[...])


def finish_chip(share, chip_u, kern_b, minus_b, total, p2, grad, out):
    rows = chip_u.shape[0]
    term = contribution(share, chip_u, kern_b[...], minus_b[...], total[:, :1], p2)
    out[...] = grad[2 * rows : 3 * rows] + term


def finish_core(share, core, kern_b, minus_b, total, p01, grad, send):
    rows = core.shape[0] - share
    term = contribution(share, core.at[:rows], kern_b[...], minus_b[...], total[:, :1], halves(share, p01)[1])
    send[...] = (grad[rows : 2 * rows] + term).astype(BF16)


def finish_own(share, whole, kern_b, minus_b, total, p01, grad, back, out):
    rows = whole.shape[0] - share
    term = contribution(share, whole.at[:rows], kern_b[...], minus_b[...], total[:, :1], halves(share, p01)[0])
    out[...] = grad[:rows] + term + back[...].astype(F32)


def sum_cores(rows, keep, lines, back, send, both):
    send[:rows] = (keep[...] + back[:rows].astype(F32)).astype(BF16)
    both[...] = lines[...] + take_values(back, rows)
    put_values(send, rows, both[...])


def sum_chips(rows, keep, far, both, grad, value):
    grad[...] = keep[...] + far[:rows].astype(F32)
    total = both[...] + take_values(far, rows)
    value[...] = total[: value.shape[0]]


def body(points, grad_weights, value_weights):
    rows, cols = points.shape
    share = rows // lax.axis_size("dim")
    piece = shape(2 * share, cols)
    part = functools.partial
    coef = value_weights.astype(F32).reshape(rows // 128, 128)

    whole, chip, cross, p0 = call(
        part(pack, share),
        [shape(rows + share, cols), piece, piece, piece],
        pltpu.with_memory_space_constraint(points, pltpu.HBM),
        pltpu.with_memory_space_constraint(grad_weights, pltpu.HBM),
        scratch=[pltpu.SemaphoreType.DMA((8,))],
        spec=ANY,
    )
    core = permute(whole, 0, 1)
    p2 = permute(chip, 0, 2)
    p3 = permute(cross, 0, 3)
    near = call(part(lay_near, share), [shape(4 * share, cols)], p0, core)[0]
    next01 = permute(near, 1, 0)
    across01 = permute(near, 4, 2)
    p3 = call(part(lay_marked, share), [shape(2 * share + 16, cols)], p3, coef, near)[0]
    p2 = call(lay_second, [piece], p2, near, flops=SPACING)[0]
    next2, next3 = permute(p2, 1, 0), permute(p3, 1, 0)
    half = permute(call(part(lay_half, share), [piece], whole, p3)[0], 0, 2)
    last01 = permute(next01, 3, 0)
    far = call(part(lay_far, share), [shape(4 * share + 16, cols)], p2, p3, across01, flops=SPACING)[0]
    across23 = permute(far, 4, 2)
    last2 = permute(next2, 3, 0)
    rest = call(part(lay_rest, share), [shape(4 * share, cols)], p2, p3, half)[0]
    rest = permute(rest, 0, 1)
    last3 = permute(next3, 3, 0)

    begun = call(
        part(begin_last, share),
        [*[shape(rows, share, F32)] * 2, *[shape(share, cols, F32)] * 2],
        whole,
        core,
        last01,
        flops=SPACING,
    )
    sums = [shape(4 * rows, cols, F32), shape(rows, 128, F32)]
    wide, column = shape(rows, cols), shape(rows, 128, F32)
    chip_u, cross_u, norm, grad, value = call(
        part(meet_own, share), [wide, wide, column, *sums], whole, core, near, p2, p3, half, rest, begun[0]
    )
    points_of = (whole, core, chip_u, cross_u)
    grad, value = call(part(meet_next, share), sums, *points_of, norm, next01, next2, next3, grad, value)
    grad, value = call(part(meet_across, share), sums, *points_of, norm, across01, across23, grad, value)
    table = shape(rows, share)
    begun = call(
        part(continue_last, share),
        [*[shape(rows, share, F32)] * 2, *[shape(share, cols, F32)] * 2],
        chip_u,
        last2,
        *begun,
    )
    send, kern, minus, total, lines = call(
        part(meet_last, share),
        [shape(rows + 16, cols), table, table, column, shape(16, 128, F32)],
        chip_u,
        cross_u,
        norm,
        last2,
        last3,
        *begun,
        grad,
        value,
    )
    back = permute(send, 0, 1)
    weights = (kern, minus, total)
    keep_chip = call(
        part(finish_chip, share), [shape(rows, cols, F32)], chip_u, *weights, last2, grad
    )[0]
    send, lines = call(
        part(sum_cores, rows), [shape(rows + 16, cols), shape(16, 128, F32)], keep_chip, lines, back
    )
    far = permute(send, 0, 2)
    send = call(part(finish_core, share), [wide], core, *weights, last01, grad)[0]
    back = permute(send, 0, 1)
    keep = call(
        part(finish_own, share), [shape(rows, cols, F32)], whole, *weights, last01, grad, back
    )[0]
    grad, value = call(
        part(sum_chips, rows), [shape(rows, cols, F32), shape(rows // 128, 128, F32)], keep, far, lines
    )
    return value.reshape(rows), grad


def solution(mesh):
    return jax.shard_map(
        body,
        mesh=mesh,
        in_specs=(P("pts", "dim"), P("pts", "dim"), P("pts")),
        out_specs=(P("pts"), P("pts", "dim")),
        check_vma=False,
    )
```

```python
import functools

import jax
import jax.numpy as jnp
from jax import lax
from jax.experimental import pallas as pl
from jax.experimental.pallas import tpu as pltpu
from jax.sharding import PartitionSpec as P

F32, BF16 = jnp.float32, jnp.bfloat16
VMEM = pl.BlockSpec(memory_space=pltpu.VMEM)
ANY = pl.BlockSpec(memory_space=pltpu.HBM)
NT = (((1,), (1,)), ((), ()))
SPACING = 2_000_000_000


def permute(array, pts, dim):
    devices_p, devices_d = lax.axis_size("pts"), lax.axis_size("dim")
    pairs = [
        (p * devices_d + d, (p ^ pts) * devices_d + (d ^ dim))
        for p in range(devices_p)
        for d in range(devices_d)
    ]
    return lax.ppermute(array, ("pts", "dim"), pairs)


def call(kernel, outs, *args, flops=0, scratch=(), spec=VMEM):
    return pl.pallas_call(
        kernel,
        out_shape=outs,
        in_specs=[spec] * len(args),
        out_specs=[VMEM] * len(outs),
        scratch_shapes=scratch,
        compiler_params=pltpu.CompilerParams(vmem_limit_bytes=16 << 20),
        cost_estimate=pl.CostEstimate(flops=flops, bytes_accessed=0, transcendentals=0),
    )(*args)


def shape(rows, cols, dtype=BF16):
    return jax.ShapeDtypeStruct((rows, cols), dtype)


def quarter(which, size):
    return pl.ds(pl.multiple_of(which * size, 16), size)


def pack(share, u, b, whole, chip, cross, own, sems):
    rows, me = u.shape[0], lax.axis_index("dim")
    upper = pl.ds(0, share)
    lower = pl.ds(share, share)
    moves = [(u, whole.at[pl.ds(0, rows)]), (b.at[quarter(me ^ 1, share)], whole.at[pl.ds(rows, share)])]
    for which, out in ((2, chip), (3, cross), (0, own)):
        moves.append((u.at[quarter(me ^ which, share)], out.at[upper]))
        moves.append((b.at[quarter(me ^ which, share)], out.at[lower]))
    copies = [pltpu.make_async_copy(*move, sems.at[n]) for n, move in enumerate(moves)]
    for copy in copies:
        copy.start()
    for copy in copies:
        copy.wait()


def lay_near(share, own, core, near):
    rows, me = core.shape[0] - share, lax.axis_index("dim")
    near[: 2 * share] = own[...]
    near[2 * share : 3 * share] = core[quarter(me, share), :]
    near[3 * share :] = core[rows:]


def lay_marked(share, cross, coef, after, piece):
    piece[: 2 * share] = cross[...]
    me, lanes = lax.axis_index("dim"), coef.shape[1]
    row = lax.broadcasted_iota(jnp.int32, coef.shape, 0)
    first, skip = me * share // lanes, me * share % lanes
    parts = [
        jnp.sum(jnp.where(row == first + n, coef[...], 0.0), 0, keepdims=True) for n in range(2)
    ]
    mine = jnp.broadcast_to(jnp.concatenate(parts, 1), (16, 2 * lanes))
    piece[2 * share :] = pltpu.roll(mine, lax.rem(2 * lanes - skip, 2 * lanes), 1).astype(BF16)


def lay_second(chip, *refs):
    refs[-1][...] = chip[...]


def lay_far(share, p2, p3, after, far):
    far[: 2 * share] = p2[...]
    far[2 * share :] = p3[...]


def lay_half(share, whole, *refs):
    half = refs[-1]
    half[...] = whole[quarter(lax.axis_index("dim") // 2, 2 * share), :]


def lay_rest(share, p2, p3, half, rest):
    rest[:share] = p2[:share]
    rest[share : 2 * share] = p3[:share]
    rest[2 * share :] = half[...]


def as_row(column):
    size = column.shape[0]
    diagonal = lax.broadcasted_iota(jnp.int32, (size, size), 0) == lax.broadcasted_iota(
        jnp.int32, (size, size), 1
    )
    return jnp.sum(jnp.where(diagonal, column, 0.0), 0, keepdims=True)


def norms_of(slices):
    total = 0.0
    for part in slices:
        wide = part.astype(F32)
        total = total + wide * wide
    return jnp.sum(total, 1, keepdims=True)


def halves(share, ref):
    return ref.at[: 2 * share], ref.at[2 * share : 4 * share]


def dots(share, own, pieces):
    gram = cross = square = inner = 0.0
    for mine, piece in zip(own, pieces):
        far_u, far_b = piece[:share], piece[share : 2 * share]
        gram = gram + lax.dot_general(mine[...], far_u, NT, preferred_element_type=F32)
        cross = cross + lax.dot_general(mine[...], far_b, NT, preferred_element_type=F32)
        far_u = far_u.astype(F32)
        square = square + far_u * far_u
        inner = inner + far_u * far_b.astype(F32)
    return gram, cross, square, inner


def weigh(share, own_norm, gram, cross, square, inner, coef):
    norm = as_row(jnp.sum(square, 1, keepdims=True))
    inner = as_row(jnp.sum(inner, 1, keepdims=True))
    coef = coef[2 * share :].astype(F32)[:1, :share]
    kern = jnp.exp(gram - 0.5 * (own_norm + norm))
    return kern, kern * (coef + cross - inner)


def meet(share, own, own_norm, pieces, coef):
    return weigh(share, own_norm, *dots(share, own, pieces), coef)


def contribution(share, own, kern_b, minus_b, value, piece):
    return (
        jnp.dot(minus_b, piece[:share], preferred_element_type=F32)
        + jnp.dot(kern_b, piece[share : 2 * share], preferred_element_type=F32)
        - own[...].astype(F32) * value
    )


def meet_own(share, *refs):
    whole, core, near, chip, cross, half, rest, after, chip_u, cross_u, norm, grad, value = refs
    rows, me = whole.shape[0] - share, lax.axis_index("dim")
    other = quarter(1 - me // 2, 2 * share)
    chip_u[quarter(me, share), :] = chip[:share]
    chip_u[quarter(me ^ 1, share), :] = rest[share : 2 * share]
    chip_u[other, :] = half[...]
    cross_u[quarter(me, share), :] = cross[:share]
    cross_u[quarter(me ^ 1, share), :] = rest[:share]
    cross_u[other, :] = rest[2 * share :]
    own = [whole[:rows], core[:rows], chip_u[...], cross_u[...]]
    own_norm = norms_of(own)
    norm[...] = jnp.broadcast_to(own_norm, norm.shape)
    pieces = [*halves(share, near), chip, cross]
    kern, minus = meet(share, own, own_norm, pieces, cross)
    total = jnp.sum(minus, 1, keepdims=True)
    value[...] = jnp.broadcast_to(total, value.shape)
    kern_b, minus_b = kern.astype(BF16), minus.astype(BF16)
    for k in range(4):
        grad[k * rows : (k + 1) * rows] = contribution(share, own[k], kern_b, minus_b, total, pieces[k])


def add_block(share, own, norm, pieces, coef, grad_in, value_in, grad, value):
    rows = norm.shape[0]
    kern, minus = meet(share, own, norm[:, :1], pieces, coef)
    total = jnp.sum(minus, 1, keepdims=True)
    value[...] = value_in[...] + total
    kern_b, minus_b = kern.astype(BF16), minus.astype(BF16)
    for k in range(4):
        at = slice(k * rows, (k + 1) * rows)
        grad[at] = grad_in[at] + contribution(share, own[k], kern_b, minus_b, total, pieces[k])


def meet_next(share, whole, core, chip_u, cross_u, norm, p01, p2, p3, grad_in, value_in, grad, value):
    rows = norm.shape[0]
    own = [whole[:rows], core[:rows], chip_u[...], cross_u[...]]
    add_block(share, own, norm, [*halves(share, p01), p2, p3], p3, grad_in, value_in, grad, value)


def meet_across(share, *refs):
    whole, core, chip_u, cross_u, norm, p01, p23, grad_in, value_in, grad, value = refs
    rows = norm.shape[0]
    own = [whole[:rows], core[:rows], chip_u[...], cross_u[...]]
    pieces = [*halves(share, p23), *halves(share, p01)]
    add_block(share, own, norm, pieces, p23.at[2 * share :], grad_in, value_in, grad, value)


def put_values(out, start, rows_of):
    high = rows_of.astype(BF16)
    low = (rows_of - high.astype(F32)).astype(BF16)
    out[start:] = jnp.concatenate([high, low], 1)


def take_values(ref, start):
    both = ref[start:].astype(F32)
    half = both.shape[1] // 2
    return both[:, :half] + both[:, half:]


def begin_last(share, whole, core, p01, *outs):
    rows = whole.shape[0] - share
    for out, value in zip(outs, dots(share, [whole[:rows], core[:rows]], halves(share, p01))):
        out[...] = value


def continue_last(share, chip_u, p2, *refs):
    more = dots(share, [chip_u], [p2])
    for out, before, value in zip(refs[-4:], refs[:4], more):
        out[...] = before[...] + value


def meet_last(share, *refs):
    chip_u, cross_u, norm, p2, p3, begun, grad, value_in, send, kern_b, minus_b, total, lines = (
        *refs[:5], refs[5:9], *refs[9:]
    )
    rows = chip_u.shape[0]
    sums = [one[...] + more for one, more in zip(begun, dots(share, [cross_u], [p3]))]
    kern, minus = weigh(share, norm[:, :1], *sums, p3)
    part = jnp.sum(minus, 1, keepdims=True)
    kern_b[...] = kern.astype(BF16)
    minus_b[...] = minus.astype(BF16)
    total[...] = jnp.broadcast_to(part, total.shape)
    term = contribution(share, cross_u, kern_b[...], minus_b[...], part, p3)
    send[:rows] = (grad[3 * rows :] + term).astype(BF16)
    value = value_in[:, :1] + part
    rows_of = [as_row(value[at : at + 128]) for at in range(0, rows, 128)]
    rows_of += [jnp.zeros_like(rows_of[0])] * (16 - len(rows_of))
    lines[...] = jnp.concatenate(rows_of, 0)
    put_values(send, rows, lines[...])


def finish_chip(share, chip_u, kern_b, minus_b, total, p2, grad, out):
    rows = chip_u.shape[0]
    term = contribution(share, chip_u, kern_b[...], minus_b[...], total[:, :1], p2)
    out[...] = grad[2 * rows : 3 * rows] + term


def finish_core(share, core, kern_b, minus_b, total, p01, grad, send):
    rows = core.shape[0] - share
    term = contribution(share, core.at[:rows], kern_b[...], minus_b[...], total[:, :1], halves(share, p01)[1])
    send[...] = (grad[rows : 2 * rows] + term).astype(BF16)


def finish_own(share, whole, kern_b, minus_b, total, p01, grad, back, out):
    rows = whole.shape[0] - share
    term = contribution(share, whole.at[:rows], kern_b[...], minus_b[...], total[:, :1], halves(share, p01)[0])
    out[...] = grad[:rows] + term + back[...].astype(F32)


def sum_cores(rows, keep, lines, back, send, both):
    send[:rows] = (keep[...] + back[:rows].astype(F32)).astype(BF16)
    both[...] = lines[...] + take_values(back, rows)
    put_values(send, rows, both[...])


def sum_chips(rows, keep, far, both, grad, value):
    grad[...] = keep[...] + far[:rows].astype(F32)
    total = both[...] + take_values(far, rows)
    value[...] = total[: value.shape[0]]


def body(points, grad_weights, value_weights):
    rows, cols = points.shape
    share = rows // lax.axis_size("dim")
    piece = shape(2 * share, cols)
    part = functools.partial
    coef = value_weights.astype(F32).reshape(rows // 128, 128)

    whole, chip, cross, p0 = call(
        part(pack, share),
        [shape(rows + share, cols), piece, piece, piece],
        pltpu.with_memory_space_constraint(points, pltpu.HBM),
        pltpu.with_memory_space_constraint(grad_weights, pltpu.HBM),
        scratch=[pltpu.SemaphoreType.DMA((8,))],
        spec=ANY,
    )
    core = permute(whole, 0, 1)
    p2 = permute(chip, 0, 2)
    p3 = permute(cross, 0, 3)
    near = call(part(lay_near, share), [shape(4 * share, cols)], p0, core)[0]
    next01 = permute(near, 1, 0)
    across01 = permute(near, 4, 2)
    p3 = call(part(lay_marked, share), [shape(2 * share + 16, cols)], p3, coef, near)[0]
    p2 = call(lay_second, [piece], p2, near, flops=SPACING)[0]
    next2, next3 = permute(p2, 1, 0), permute(p3, 1, 0)
    half = permute(call(part(lay_half, share), [piece], whole, p3)[0], 0, 2)
    last01 = permute(next01, 3, 0)
    far = call(part(lay_far, share), [shape(4 * share + 16, cols)], p2, p3, across01, flops=SPACING)[0]
    across23 = permute(far, 4, 2)
    last2 = permute(next2, 3, 0)
    rest = call(part(lay_rest, share), [shape(4 * share, cols)], p2, p3, half)[0]
    rest = permute(rest, 0, 1)
    last3 = permute(next3, 3, 0)

    begun = call(
        part(begin_last, share),
        [*[shape(rows, share, F32)] * 2, *[shape(share, cols, F32)] * 2],
        whole,
        core,
        last01,
        flops=SPACING,
    )
    sums = [shape(4 * rows, cols, F32), shape(rows, 128, F32)]
    wide, column = shape(rows, cols), shape(rows, 128, F32)
    chip_u, cross_u, norm, grad, value = call(
        part(meet_own, share), [wide, wide, column, *sums], whole, core, near, p2, p3, half, rest, begun[0]
    )
    points_of = (whole, core, chip_u, cross_u)
    grad, value = call(part(meet_next, share), sums, *points_of, norm, next01, next2, next3, grad, value)
    grad, value = call(part(meet_across, share), sums, *points_of, norm, across01, across23, grad, value)
    table = shape(rows, share)
    begun = call(
        part(continue_last, share),
        [*[shape(rows, share, F32)] * 2, *[shape(share, cols, F32)] * 2],
        chip_u,
        last2,
        *begun,
        value,
    )
    send, kern, minus, total, lines = call(
        part(meet_last, share),
        [shape(rows + 16, cols), table, table, column, shape(16, 128, F32)],
        chip_u,
        cross_u,
        norm,
        last2,
        last3,
        *begun,
        grad,
        value,
    )
    back = permute(send, 0, 1)
    weights = (kern, minus, total)
    keep_chip = call(
        part(finish_chip, share), [shape(rows, cols, F32)], chip_u, *weights, last2, grad
    )[0]
    send, lines = call(
        part(sum_cores, rows), [shape(rows + 16, cols), shape(16, 128, F32)], keep_chip, lines, back
    )
    far = permute(send, 0, 2)
    send = call(part(finish_core, share), [wide], core, *weights, last01, grad)[0]
    back = permute(send, 0, 1)
    keep = call(
        part(finish_own, share), [shape(rows, cols, F32)], whole, *weights, last01, grad, back
    )[0]
    grad, value = call(
        part(sum_chips, rows), [shape(rows, cols, F32), shape(rows // 128, 128, F32)], keep, far, lines
    )
    return value.reshape(rows), grad


def solution(mesh):
    return jax.shard_map(
        body,
        mesh=mesh,
        in_specs=(P("pts", "dim"), P("pts", "dim"), P("pts")),
        out_specs=(P("pts"), P("pts", "dim")),
        check_vma=False,
    )
```
